256 devices in a mesh: samples: 4 (over y), channel: 32 (over z, x), spatial: 2 (over core).
Axes of the slice: x: 4, y: 4, z: 8, core: 2. Of those that a mesh axis runs over, the one named last changes fastest.
Arguments:
- features: bfloat16 [512, 4, 2, 1024], P('channel', 'samples', 'spatial'), may hold values from -6 to 6
- conv_one: bfloat16 [27, 512, 512], P(None, 'channel'), may hold values from -0.09375 to 0.09375
- conv_two: bfloat16 [27, 512, 512], P(None, 'channel'), may hold values from -0.09375 to 0.09375
- cotangent: bfloat16 [512, 4, 2, 1024], P('channel', 'samples', 'spatial'), may hold values from -6 to 6
Outputs:
- mixed_out: bfloat16 [512, 4, 2, 1024], P('channel', 'samples', 'spatial')
- input_grad: bfloat16 [512, 4, 2, 1024], P('channel', 'samples', 'spatial')
- grad_one: float32 [27, 512, 512], P(None, 'channel')
- grad_two: float32 [27, 512, 512], P(None, 'channel')
The draws below stay inside these ranges and needn't reach their ends.
All inputs are finite; a program needn't handle non-finite values.
Results may differ from the reference program's by a relative error of at most 0.017.
Values may be sent and summed in bfloat16 or wider, within the bound.
No kernel may reach another device: no remote copies, remote signals or barrier semaphores. Data moves between devices by JAX's collectives and lax.ppermute only.
A program may use at most 64 MiB of HBM per device.

```python
import jax
import jax.numpy as jnp
from jax import lax

C = 512
SIDE = 32
CROPS = 4
DEPTH = 2
PLANE = 1024


def spiked(values, key, source, target, blocks, factor):
    owner, partner = [(jnp.arange(values.shape[position]) // (values.shape[position] // blocks)).reshape([-1 if axis == position else 1 for axis in range(values.ndim)]) for position in (source, target)]
    chosen = jax.random.permutation(key, blocks)[partner]
    strong = (owner == chosen) | (owner == (partner + blocks // 2) % blocks)
    return jnp.where(strong, factor * values, values)


def level_of(stream_key, dims, split, low, top_value):
    level = 1.0
    for position, shards_of in split:
        draws = jax.random.uniform(jax.random.fold_in(jax.random.fold_in(stream_key, 6), position), (shards_of,), jnp.float32, low / len(split), top_value / len(split))
        level = level * jnp.repeat(jnp.exp(draws), dims[position] // shards_of).reshape((-1,) + (1,) * (len(dims) - 1 - position))
    return level


def scatter_about(own_key, shape, deviation, limit, shards=(), held_as=jnp.bfloat16):
    loudness = level_of(own_key, shape, shards, -0.22, 0.18) if shards else 1.0
    values = jax.random.normal(own_key, shape, jnp.float32) * deviation * loudness
    return jnp.minimum(jnp.maximum(values, -limit), limit).astype(held_as)


def noise_with(stream_key, extent, spread, limit, split, heavy, held_as=jnp.bfloat16):
    drawn = spread * jax.random.normal(stream_key, extent, jnp.float32)
    if split:
        drawn = drawn * level_of(stream_key, extent, split, -0.22, 0.18)
    return jnp.clip(spiked(drawn, jax.random.fold_in(stream_key, 3), *heavy), -limit, limit).astype(held_as)


def setup_inputs(seed: int = 0) -> dict:
    streams_of = jax.random.split(jax.random.key(seed), 5)
    features = scatter_about(streams_of[0], (C, CROPS, DEPTH, PLANE), 1.0, 6.0, ((0, 32), (1, 4), (2, 2)))
    conv_one = noise_with(streams_of[1], (27, C, C), (27 * C) ** -0.5, 0.09375, ((1, 32),), (1, 2, 32, 2.75))
    conv_two = noise_with(streams_of[2], (27, C, C), (27 * C) ** -0.5, 0.09375, ((1, 32),), (1, 2, 32, 2.75))
    cotangent = scatter_about(streams_of[3], (C, CROPS, DEPTH, PLANE), 1.0, 6.0, ((0, 32), (1, 4), (2, 2)))
    return {"features": features, "conv_one": conv_one, "conv_two": conv_two, "cotangent": cotangent}


def to_grid(values):
    return values.reshape(values.shape[0], values.shape[1], values.shape[2], SIDE, SIDE)

def to_flat(values):
    return values.reshape(values.shape[0], values.shape[1], values.shape[2], SIDE * SIDE)

def as_taps(kernel):
    return kernel.reshape(3, 3, 3, kernel.shape[1], kernel.shape[2])

def forward_conv(source, kernel, rhs_spec, depth_pad):
    return lax.conv_general_dilated(source, as_taps(kernel), (1, 1, 1), [(depth_pad, depth_pad), (1, 1), (1, 1)], dimension_numbers=('CNDHW', rhs_spec, 'CNDHW'), preferred_element_type=jnp.float32)

def data_grad(source, kernel, rhs_spec, depth_pad):
    flipped = as_taps(kernel)[::-1, ::-1, ::-1]
    return lax.conv_general_dilated(source, flipped, (1, 1, 1), [(depth_pad, depth_pad), (1, 1), (1, 1)], dimension_numbers=('CNDHW', rhs_spec, 'CNDHW'), preferred_element_type=jnp.float32)

def weight_grad(padded, upstream, out_spec):
    result = lax.conv_general_dilated(padded, upstream, (1, 1, 1), [(0, 0), (0, 0), (0, 0)], dimension_numbers=('NCDHW', 'OIDHW', out_spec), preferred_element_type=jnp.float32)
    return result.reshape(27, result.shape[3], result.shape[4])

def reference(features, conv_one, conv_two, cotangent):
    source = to_grid(features)
    upstream = to_grid(cotangent)
    pre_act = forward_conv(source, conv_one, 'DHWOI', 1)
    hidden = jax.nn.silu(pre_act).astype(jnp.bfloat16)
    mixed_out = forward_conv(hidden, conv_two, 'DHWIO', 1).astype(jnp.bfloat16)
    hidden_grad = data_grad(upstream, conv_two, 'DHWOI', 1)
    sigmoid_v = jax.nn.sigmoid(pre_act)
    act_grad = (hidden_grad * sigmoid_v * (1.0 + pre_act * (1.0 - sigmoid_v))).astype(jnp.bfloat16)
    input_grad = data_grad(act_grad, conv_one, 'DHWIO', 1).astype(jnp.bfloat16)
    widths = ((0, 0), (0, 0), (1, 1), (1, 1), (1, 1))
    grad_two = weight_grad(jnp.pad(hidden, widths), upstream, 'DHWNC')
    grad_one = weight_grad(jnp.pad(source, widths), act_grad, 'DHWCN')
    return (to_flat(mixed_out), to_flat(input_grad), grad_one, grad_two)
```

```python
import jax
import jax.numpy as jnp
from jax import lax
from jax.experimental import pallas as pl
from jax.experimental.pallas import tpu as pltpu
from jax.sharding import PartitionSpec as P

SIDE = 32
PLANE = SIDE * SIDE
TAPS9 = [(b, c) for b in range(3) for c in range(3)]
F32 = jnp.float32
BF16 = jnp.bfloat16
PARAMS = pltpu.CompilerParams(vmem_limit_bytes=48 * 1024 * 1024)


def masks(rows):
    cell = lax.broadcasted_iota(jnp.int32, (rows, PLANE), 1)
    column = cell & (SIDE - 1)
    row_ok = {-1: cell >= SIDE, 1: cell < PLANE - SIDE}
    col_ok = {-1: column > 0, 1: column < SIDE - 1}
    return row_ok, col_ok


def moved(values, step, ok):
    return jnp.where(ok, pltpu.roll(values, (-step) % PLANE, 1), 0.0)


def dot(lhs, rhs, dims):
    return lax.dot_general(lhs, rhs, (dims, ((), ())), preferred_element_type=F32)


def tap_sum(stack_ref, start, width, sign, ok):
    row_ok, col_ok = ok
    total = None
    for c in range(3):
        part = None
        for b in range(3):
            at = start + (3 * b + c) * width
            term = stack_ref[at : at + width, :]
            drow = sign * (b - 1)
            if drow:
                term = moved(term, SIDE * drow, row_ok[drow])
            part = term if part is None else part + term
        dcol = sign * (c - 1)
        if dcol:
            part = moved(part, dcol, col_ok[dcol])
        total = part if total is None else total + part
    return total


def first_kernel(core_ref, whole_ref, one_ref, two_ref, out_ref, near, far):
    blocks, _, width, _ = whole_ref.shape
    third = 9 * width
    ok = masks(width)

    def run(weights, sign):
        source = [whole_ref[:, d].reshape(blocks * width, PLANE) for d in range(2)]
        low, high = weights[0 : 2 * third, :], weights[third : 3 * third, :]
        left, right = (low, high) if sign > 0 else (high, low)
        near[...] = dot(left, source[0], ((1,), (0,)))
        far[...] = dot(right, source[1], ((1,), (0,)))
        near[...] = near[...] + far[...]
        for d in range(2):
            start = third * ((1 - d) if sign > 0 else d)
            out_ref[d] = tap_sum(near, start, width, sign, ok)

    @pl.when(core_ref[0] == 0)
    def _():
        run(one_ref, 1)

    @pl.when(core_ref[0] == 1)
    def _():
        run(two_ref, -1)


def spread(values, sign, col_ref, start, ok):
    row_ok, col_ok = ok
    width = values.shape[0]
    for c in range(3):
        dcol = sign * (c - 1)
        part = moved(values, dcol, col_ok[dcol]) if dcol else values
        for b in range(3):
            drow = sign * (b - 1)
            term = moved(part, SIDE * drow, row_ok[drow]) if drow else part
            at = start + (3 * b + c) * width
            col_ref[at : at + width, :] = term.astype(BF16)


def second_kernel(core_ref, own_ref, other_ref, whole_ref, one_ref, two_ref, out_ref, grad_ref, hid_col, act_col):
    blocks, _, width, _ = whole_ref.shape
    third = 9 * width
    channels = blocks * width
    ok = masks(width)
    first = core_ref[0] == 0
    for d in range(2):
        own, other = own_ref[d], other_ref[d]
        pre = jnp.where(first, own, other)
        upstream = jnp.where(first, other, own)
        gate = 1.0 / (1.0 + jnp.exp(-pre))
        hidden = (pre * gate).astype(BF16).astype(F32)
        act = (upstream * gate * (1.0 + pre * (1.0 - gate))).astype(BF16).astype(F32)
        spread(hidden, 1, hid_col, d * third, ok)
        spread(act, -1, act_col, (1 - d) * third, ok)

    def run(weights, out_col, grad_col, sign):
        for d in range(2):
            at = third * ((1 - d) if sign > 0 else d)
            part = dot(weights[at : at + 2 * third, :], out_col[...], ((0,), (0,)))
            out_ref[:, d] = part.astype(BF16).reshape(blocks, width, PLANE)
        source = [whole_ref[:, d].reshape(channels, PLANE) for d in range(2)]
        zero = dot(grad_col[...], source[0], ((1,), (1,)))
        last = dot(grad_col[...], source[1], ((1,), (1,)))
        low, high = (zero, last) if sign > 0 else (last, zero)
        grad_ref[0:third, :] = low[0:third].astype(BF16)
        grad_ref[third : 2 * third, :] = (low[third:] + high[0:third]).astype(BF16)
        grad_ref[2 * third :, :] = high[third:].astype(BF16)

    @pl.when(first)
    def _():
        run(two_ref, hid_col, act_col, 1)

    @pl.when(core_ref[0] == 1)
    def _():
        run(one_ref, act_col, hid_col, -1)


def vmem(count):
    return [pl.BlockSpec(memory_space=pltpu.VMEM)] * count


def smem():
    return [pl.BlockSpec(memory_space=pltpu.SMEM)]


def first_call(core, whole, one, two):
    width = whole.shape[2]
    return pl.pallas_call(
        first_kernel,
        out_shape=jax.ShapeDtypeStruct((2, width, PLANE), F32),
        in_specs=smem() + vmem(3),
        out_specs=vmem(1)[0],
        scratch_shapes=[pltpu.VMEM((18 * width, PLANE), F32)] * 2,
        compiler_params=PARAMS,
        name="conv_in",
    )(core, whole, one, two)


def second_call(core, own, other, whole, one, two):
    blocks, _, width, _ = whole.shape
    return pl.pallas_call(
        second_kernel,
        out_shape=(
            jax.ShapeDtypeStruct(whole.shape, BF16),
            jax.ShapeDtypeStruct((27 * width, blocks * width), BF16),
        ),
        in_specs=smem() + vmem(5),
        out_specs=tuple(vmem(2)),
        scratch_shapes=[pltpu.VMEM((18 * width, PLANE), BF16)] * 2,
        compiler_params=PARAMS,
        name="conv_out",
    )(core, own, other, whole, one, two)


def swap(values):
    return lax.ppermute(values, "spatial", [(0, 1), (1, 0)])


def around(values, axis, step):
    size = lax.axis_size(axis)
    return lax.ppermute(values, axis, [(i, (i + step) % size) for i in range(size)])


def body(features, conv_one, conv_two, cotangent):
    width, channels = conv_one.shape[1], conv_one.shape[2]
    count = lax.axis_size("channel")
    core = lax.axis_index("spatial")
    first = core == 0
    flag = core.astype(jnp.int32).reshape(1)
    one = conv_one.reshape(27 * width, channels)
    two = conv_two.reshape(27 * width, channels)
    features = features.reshape(width, PLANE)
    cotangent = cotangent.reshape(width, PLANE)

    came = swap(jnp.where(first, cotangent, features))
    kept = jnp.where(first, features, cotangent)
    block = jnp.where(first, jnp.stack([kept, came]), jnp.stack([came, kept]))
    whole = lax.all_to_all(
        jnp.broadcast_to(block, (count,) + block.shape), "channel", 0, 0, tiled=True
    )
    own = first_call(flag, whole, one, two)
    other = swap(own)
    parts, grad = second_call(flag, own, other, whole, one, two)

    grads = [grad] + [around(grad, "samples", k) for k in (1, 2, 3)]
    summed = sum(g.astype(F32) for g in grads).astype(BF16)
    summed_other = swap(summed)

    parts = lax.all_to_all(parts, "channel", 0, 0, tiled=True)
    result = jnp.sum(parts.astype(F32), axis=0).astype(BF16)
    mine = jnp.where(first, result[0], result[1])
    theirs = swap(jnp.where(first, result[1], result[0]))
    shape = (width, 1, 1, PLANE)
    mixed_out = jnp.where(first, mine, theirs).reshape(shape)
    input_grad = jnp.where(first, theirs, mine).reshape(shape)
    grad_one = jnp.where(first, summed, summed_other).astype(F32).reshape(27, width, channels)
    grad_two = jnp.where(first, summed_other, summed).astype(F32).reshape(27, width, channels)
    return mixed_out, input_grad, grad_one, grad_two


def solution(mesh):
    acts = P("channel", "samples", "spatial", None)
    kernels = P(None, "channel", None)
    return jax.shard_map(
        body,
        mesh=mesh,
        in_specs=(acts, kernels, kernels, acts),
        out_specs=(acts, acts, kernels, kernels),
        check_vma=False,
    )
```

```python
import jax
import jax.numpy as jnp
from jax import lax
from jax.experimental import pallas as pl
from jax.experimental.pallas import tpu as pltpu
from jax.sharding import Mesh, PartitionSpec as P

SIDE = 32
PLANE = SIDE * SIDE
F32 = jnp.float32
BF16 = jnp.bfloat16
PARAMS = pltpu.CompilerParams(vmem_limit_bytes=40 * 1024 * 1024)
NX = 4
NZ = 8


def masks(rows):
    cell = lax.broadcasted_iota(jnp.int32, (rows, PLANE), 1)
    column = cell & (SIDE - 1)
    row_ok = {-1: cell >= SIDE, 1: cell < PLANE - SIDE}
    col_ok = {-1: column > 0, 1: column < SIDE - 1}
    return row_ok, col_ok


def moved(values, step, ok):
    return jnp.where(ok, pltpu.roll(values, (-step) % PLANE, 1), 0.0)


def dot(lhs, rhs, dims):
    return lax.dot_general(lhs, rhs, (dims, ((), ())), preferred_element_type=F32)


def tap_sum(stack_ref, start, width, sign, ok):
    row_ok, col_ok = ok
    total = None
    for c in range(3):
        part = None
        for b in range(3):
            at = start + (3 * b + c) * width
            term = stack_ref[at : at + width, :]
            drow = sign * (b - 1)
            if drow:
                term = moved(term, SIDE * drow, row_ok[drow])
            part = term if part is None else part + term
        dcol = sign * (c - 1)
        if dcol:
            part = moved(part, dcol, col_ok[dcol])
        total = part if total is None else total + part
    return total


def spread(values, sign, col_ref, start, ok):
    row_ok, col_ok = ok
    width = values.shape[0]
    for c in range(3):
        dcol = sign * (c - 1)
        part = moved(values, dcol, col_ok[dcol]) if dcol else values
        for b in range(3):
            drow = sign * (b - 1)
            term = moved(part, SIDE * drow, row_ok[drow]) if drow else part
            at = start + (3 * b + c) * width
            col_ref[at : at + width, :] = term.astype(BF16)


def regroup_kernel(at_ref, one_ref, two_ref, out_ref):
    channels = one_ref.shape[1]
    width = channels // (NX * NZ)
    group = NZ * width
    old = lax.broadcasted_iota(jnp.int32, (channels, channels), 0)
    new = lax.broadcasted_iota(jnp.int32, (channels, channels), 1)
    home = ((new % group) // width) * (NX * width) + (new // group) * width + new % width
    order = (old == home).astype(F32).astype(BF16)

    def run(ref):
        for x in range(NX):
            out_ref[x] = dot(ref[...], order[:, x * group : (x + 1) * group], ((1,), (0,))).astype(BF16)

    @pl.when(at_ref[0] == 0)
    def _():
        run(two_ref)

    @pl.when(at_ref[0] == 1)
    def _():
        run(one_ref)


def first_kernel(at_ref, mine_ref, left_ref, right_ref, far0_ref, far1_ref, one_ref, two_ref, out_ref, whole_ref, near, far):
    width = mine_ref.shape[2]
    third = 9 * width
    ok = masks(width)
    x = at_ref[1]
    half = NZ // 2
    pieces = ((mine_ref, 0, 0, NZ), (left_ref, NX - 1, 0, NZ), (right_ref, 1, 0, NZ), (far0_ref, 2, 0, half), (far1_ref, 2, half, half))
    for ref, step, z0, count in pieces:
        source = lax.rem(x + step, NX)
        for z in range(count):
            rows = pl.ds(pl.multiple_of(((z0 + z) * NX + source) * width, 16), width)
            for d in range(2):
                whole_ref[d, rows, :] = ref[z, d]

    def run(weights, sign):
        low, high = weights[0 : 2 * third, :], weights[third : 3 * third, :]
        first, second = (low, high) if sign > 0 else (high, low)
        near[...] = dot(first, whole_ref[0], ((1,), (0,)))
        far[...] = dot(second, whole_ref[1], ((1,), (0,)))
        near[...] = near[...] + far[...]
        for d in range(2):
            start = third * ((1 - d) if sign > 0 else d)
            out_ref[d] = tap_sum(near, start, width, sign, ok)

    @pl.when(at_ref[0] == 0)
    def _():
        run(one_ref, 1)

    @pl.when(at_ref[0] == 1)
    def _():
        run(two_ref, -1)


def act_kernel(at_ref, own_ref, other_ref, send_ref, keep_ref):
    first = at_ref[0] == 0
    for d in range(2):
        own, other = own_ref[d], other_ref[d]
        pre = jnp.where(first, own, other)
        upstream = jnp.where(first, other, own)
        gate = 1.0 / (1.0 + jnp.exp(-pre))
        hidden = pre * gate
        act = upstream * gate * (1.0 + pre * (1.0 - gate))
        send_ref[d] = jnp.where(first, hidden, act).astype(BF16)
        keep_ref[d] = jnp.where(first, act, hidden).astype(BF16)


def grad_kernel(at_ref, keep_ref, whole_ref, grad_ref, col):
    width = keep_ref.shape[1]
    third = 9 * width
    ok = masks(width)

    def run(sign):
        for d in range(2):
            at = third * (d if sign > 0 else 1 - d)
            spread(keep_ref[d].astype(F32), sign, col, at, ok)
        zero = dot(col[...], whole_ref[0], ((1,), (1,)))
        last = dot(col[...], whole_ref[1], ((1,), (1,)))
        low, high = (last, zero) if sign > 0 else (zero, last)
        grad_ref[0:third, :] = low[0:third].astype(BF16)
        grad_ref[third : 2 * third, :] = (low[third:] + high[0:third]).astype(BF16)
        grad_ref[2 * third :, :] = high[third:].astype(BF16)

    @pl.when(at_ref[0] == 0)
    def _():
        run(-1)

    @pl.when(at_ref[0] == 1)
    def _():
        run(1)


def second_kernel(at_ref, *refs):
    acts, kernels, (out_ref, col, tall) = refs[:NX], refs[NX : 2 * NX], refs[2 * NX :]
    width = acts[0].shape[1]
    third = 9 * width
    ok = masks(width)

    def run(sign):
        for k in range(NX):
            for d in range(2):
                at = 2 * third * k + third * (d if sign > 0 else 1 - d)
                spread(acts[k][d].astype(F32), sign, col, at, ok)
        for d in range(2):
            at = third * ((1 - d) if sign > 0 else d)
            for k in range(NX):
                tall[2 * third * k : 2 * third * (k + 1), :] = kernels[k][at : at + 2 * third, :]
            part = dot(tall[...], col[...], ((0,), (0,)))
            out_ref[:, d] = part.astype(BF16).reshape(NZ, width, PLANE)

    @pl.when(at_ref[0] == 0)
    def _():
        run(1)

    @pl.when(at_ref[0] == 1)
    def _():
        run(-1)


def call(kernel, outs, scratch, name, cost, *args):
    vmem = pl.BlockSpec(memory_space=pltpu.VMEM)
    return pl.pallas_call(
        kernel,
        out_shape=tuple(jax.ShapeDtypeStruct(s, t) for s, t in outs),
        in_specs=[pl.BlockSpec(memory_space=pltpu.SMEM)] + [vmem] * (len(args) - 1),
        out_specs=tuple([vmem] * len(outs)),
        scratch_shapes=[pltpu.VMEM(s, t) for s, t in scratch],
        compiler_params=PARAMS,
        cost_estimate=pl.CostEstimate(flops=cost, bytes_accessed=0, transcendentals=0),
        name=name,
    )(*args)


def swap(values):
    return lax.ppermute(values, "spatial", [(0, 1), (1, 0)])


def around(values, axis, step):
    size = lax.axis_size(axis)
    return lax.ppermute(values, axis, [((i + step) % size, i) for i in range(size)])


def body(features, conv_one, conv_two, cotangent):
    width, channels = conv_one.shape[1], conv_one.shape[2]
    core = lax.axis_index("spatial")
    x = lax.axis_index("x")
    first = core == 0
    at = jnp.stack([core, x]).astype(jnp.int32)
    one = conv_one.reshape(27 * width, channels)
    two = conv_two.reshape(27 * width, channels)
    features = features.reshape(width, PLANE)
    cotangent = cotangent.reshape(width, PLANE)
    taps = 27 * width
    group = NZ * width

    came = swap(jnp.where(first, cotangent, features))
    kept = jnp.where(first, features, cotangent)
    block = jnp.where(first, jnp.stack([kept, came]), jnp.stack([came, kept]))
    mine = lax.all_to_all(jnp.broadcast_to(block, (NZ,) + block.shape), "z", 0, 0, tiled=True)

    (groups,) = call(regroup_kernel, [((NX, taps, group), BF16)], [], "regroup", 2 * taps * channels * channels, at, one, two)

    def group_for(step):
        return lax.dynamic_index_in_dim(groups, lax.rem(x + step, NX), 0, keepdims=False)

    kernels = [group_for(0)] + [around(group_for(NX - k), "x", k) for k in range(1, NX)]

    left = around(mine, "x", -1)
    right = around(mine, "x", 1)
    far0 = around(left[: NZ // 2], "x", -1)
    far1 = around(right[NZ // 2 :], "x", 1)

    plane = (2, width, PLANE)
    own, whole = call(
        first_kernel,
        [(plane, F32), ((2, channels, PLANE), BF16)],
        [((18 * width, PLANE), F32)] * 2,
        "conv_in",
        4 * 18 * width * channels * PLANE,
        at, mine, left, right, far0, far1, one, two,
    )
    other = swap(own)
    send, keep = call(act_kernel, [(plane, BF16)] * 2, [], "act", 0, at, own, other)
    acts = [send] + [around(send, "x", k) for k in range(1, NX)]
    (grad,) = call(
        grad_kernel,
        [((taps, channels), BF16)],
        [((18 * width, PLANE), BF16)],
        "grad",
        4 * 18 * width * channels * PLANE,
        at, keep, whole,
    )
    (parts,) = call(
        second_kernel,
        [((NZ,) + plane, BF16)],
        [((NX * 18 * width, PLANE), BF16), ((NX * 18 * width, group), BF16)],
        "conv_out",
        4 * 18 * width * channels * PLANE,
        at, *acts, *kernels,
    )
    parts = lax.all_to_all(parts, "z", 0, 0, tiled=True)

    grads = [grad] + [around(grad, "samples", k) for k in (1, 2, 3)]
    summed = sum(g.astype(F32) for g in grads).astype(BF16)
    summed_other = swap(summed)

    result = jnp.sum(parts.astype(F32), axis=0).astype(BF16)
    ours = jnp.where(first, result[0], result[1])
    theirs = swap(jnp.where(first, result[1], result[0]))
    shape = (width, 1, 1, PLANE)
    mixed_out = jnp.where(first, ours, theirs).reshape(shape)
    input_grad = jnp.where(first, theirs, ours).reshape(shape)
    grad_one = jnp.where(first, summed, summed_other).astype(F32).reshape(27, width, channels)
    grad_two = jnp.where(first, summed_other, summed).astype(F32).reshape(27, width, channels)
    return mixed_out, input_grad, grad_one, grad_two


def solution(mesh):
    fine = Mesh(
        mesh.devices.reshape(mesh.shape["samples"], NZ, NX, mesh.shape["spatial"]),
        ("samples", "z", "x", "spatial"),
    )
    acts = P(("z", "x"), "samples", "spatial", None)
    kernels = P(None, ("z", "x"), None)
    return jax.shard_map(
        body,
        mesh=fine,
        in_specs=(acts, kernels, kernels, acts),
        out_specs=(acts, acts, kernels, kernels),
        check_vma=False,
    )
```

```python
import jax
import jax.numpy as jnp
from jax import lax
from jax.experimental import pallas as pl
from jax.experimental.pallas import tpu as pltpu
from jax.sharding import Mesh, PartitionSpec as P

SIDE = 32
PLANE = SIDE * SIDE
F32 = jnp.float32
BF16 = jnp.bfloat16
PARAMS = pltpu.CompilerParams(vmem_limit_bytes=40 * 1024 * 1024)
NX = 4
NZ = 8


def masks(rows):
    cell = lax.broadcasted_iota(jnp.int32, (rows, PLANE), 1)
    column = cell & (SIDE - 1)
    row_ok = {-1: cell >= SIDE, 1: cell < PLANE - SIDE}
    col_ok = {-1: column > 0, 1: column < SIDE - 1}
    return row_ok, col_ok


def moved(values, step, ok):
    return jnp.where(ok, pltpu.roll(values, (-step) % PLANE, 1), 0.0)


def dot(lhs, rhs, dims):
    return lax.dot_general(lhs, rhs, (dims, ((), ())), preferred_element_type=F32)


def tap_sum(stack_ref, start, width, sign, ok):
    row_ok, col_ok = ok
    total = None
    for c in range(3):
        part = None
        for b in range(3):
            at = start + (3 * b + c) * width
            term = stack_ref[at : at + width, :]
            drow = sign * (b - 1)
            if drow:
                term = moved(term, SIDE * drow, row_ok[drow])
            part = term if part is None else part + term
        dcol = sign * (c - 1)
        if dcol:
            part = moved(part, dcol, col_ok[dcol])
        total = part if total is None else total + part
    return total


def spread(values, sign, col_ref, start, ok):
    row_ok, col_ok = ok
    width = values.shape[0]
    for c in range(3):
        dcol = sign * (c - 1)
        part = moved(values, dcol, col_ok[dcol]) if dcol else values
        for b in range(3):
            drow = sign * (b - 1)
            term = moved(part, SIDE * drow, row_ok[drow]) if drow else part
            at = start + (3 * b + c) * width
            col_ref[at : at + width, :] = term.astype(BF16)


def regroup_kernel(at_ref, one_ref, two_ref, *out_refs):
    channels = one_ref.shape[1]
    width = channels // (NX * NZ)
    group = NZ * width
    old = lax.broadcasted_iota(jnp.int32, (channels, group), 0)
    new = lax.broadcasted_iota(jnp.int32, (channels, group), 1)

    def run(ref):
        for k in range(NX):
            x = lax.rem(at_ref[1] + k, NX)
            home = (new // width) * (NX * width) + x * width + new % width
            order = (old == home).astype(F32).astype(BF16)
            out_refs[k][...] = dot(ref[...], order, ((1,), (0,))).astype(BF16)

    @pl.when(at_ref[0] == 0)
    def _():
        run(one_ref)

    @pl.when(at_ref[0] == 1)
    def _():
        run(two_ref)


def first_kernel(at_ref, mine_ref, *refs):
    kernels, own_ref, out_refs = refs[:NX], refs[NX], refs[NX + 1 : 2 * NX]
    all_ref, lhs, rhs, stack = refs[2 * NX :]
    width = mine_ref.shape[2]
    group = NZ * width
    third = 9 * width
    ok = masks(width)
    for d in range(2):
        rhs[d * group : (d + 1) * group, :] = mine_ref[:, d].reshape(group, PLANE)
    for k in range(NX):
        all_ref[k] = kernels[k][...]

    def run(sign):
        for d in range(2):
            for k in range(NX):
                for e in range(2):
                    a = 1 + sign * (e - d)
                    lhs[k * third : (k + 1) * third, e * group : (e + 1) * group] = kernels[k][a * third : (a + 1) * third, :]
            stack[...] = dot(lhs[...], rhs[...], ((1,), (0,)))
            for k in range(NX):
                total = tap_sum(stack, k * third, width, sign, ok)
                if k:
                    out_refs[k - 1][d] = total.astype(BF16)
                else:
                    own_ref[d] = total

    @pl.when(at_ref[0] == 0)
    def _():
        run(1)

    @pl.when(at_ref[0] == 1)
    def _():
        run(-1)


def act_kernel(at_ref, own_ref, other_ref, send_ref, keep_ref):
    first = at_ref[0] == 0
    for d in range(2):
        own, other = own_ref[d], other_ref[d]
        pre = jnp.where(first, own, other)
        upstream = jnp.where(first, other, own)
        gate = 1.0 / (1.0 + jnp.exp(-pre))
        hidden = pre * gate
        act = upstream * gate * (1.0 + pre * (1.0 - gate))
        send_ref[d] = jnp.where(first, hidden, act).astype(BF16)
        keep_ref[d] = jnp.where(first, act, hidden).astype(BF16)


def grad_kernel(at_ref, keep_ref, mine_ref, left_ref, right_ref, far0_ref, far1_ref, *refs):
    out_refs, (whole, col, full) = refs[:4], refs[4:]
    width = keep_ref.shape[1]
    third = 9 * width
    ok = masks(width)
    x = at_ref[1]
    half = NZ // 2
    pieces = ((mine_ref, 0, 0, NZ), (left_ref, NX - 1, 0, NZ), (right_ref, 1, 0, NZ), (far0_ref, 2, 0, half), (far1_ref, 2, half, half))
    for ref, step, z0, count in pieces:
        source = lax.rem(x + step, NX)
        for z in range(count):
            rows = pl.ds(pl.multiple_of(((z0 + z) * NX + source) * width, 16), width)
            for d in range(2):
                whole[d, rows, :] = ref[z, d]

    def run(sign):
        for d in range(2):
            at = third * (d if sign > 0 else 1 - d)
            spread(keep_ref[d].astype(F32), sign, col, at, ok)
        zero = dot(col[...], whole[0], ((1,), (1,)))
        last = dot(col[...], whole[1], ((1,), (1,)))
        low, high = (last, zero) if sign > 0 else (zero, last)
        full[0:third, :] = low[0:third].astype(BF16)
        full[third : 2 * third, :] = (low[third:] + high[0:third]).astype(BF16)
        full[2 * third :, :] = high[third:].astype(BF16)

    @pl.when(at_ref[0] == 0)
    def _():
        run(-1)

    @pl.when(at_ref[0] == 1)
    def _():
        run(1)

    quarter = full.shape[1] // 4
    for k in range(4):
        columns = pl.ds(pl.multiple_of(lax.rem(at_ref[2] + k, 4) * quarter, quarter), quarter)
        out_refs[k][...] = full[:, columns]


def finish_kernel(at_ref, *refs):
    own_refs, other_ref, (one_ref, two_ref) = refs[:4], refs[4], refs[5:]
    quarter = other_ref.shape[2]

    def run(own_out, other_out):
        for k in range(4):
            columns = pl.ds(pl.multiple_of(lax.rem(at_ref[2] + k, 4) * quarter, quarter), quarter)
            own_out[:, columns] = own_refs[k][...].astype(F32)
            other_out[:, columns] = other_ref[k].astype(F32)

    @pl.when(at_ref[0] == 0)
    def _():
        run(one_ref, two_ref)

    @pl.when(at_ref[0] == 1)
    def _():
        run(two_ref, one_ref)


def second_kernel(at_ref, *refs):
    acts, kernels, (out_ref, col, tall) = refs[:NX], refs[NX], refs[NX + 1 :]
    width = acts[0].shape[1]
    third = 9 * width
    ok = masks(width)

    def run(sign):
        for k in range(NX):
            for d in range(2):
                at = 2 * third * k + third * (d if sign > 0 else 1 - d)
                spread(acts[k][d].astype(F32), sign, col, at, ok)
        for d in range(2):
            at = third * ((1 - d) if sign > 0 else d)
            for k in range(NX):
                tall[2 * third * k : 2 * third * (k + 1), :] = kernels[k, at : at + 2 * third, :]
            part = dot(tall[...], col[...], ((0,), (0,)))
            out_ref[:, d] = part.astype(BF16).reshape(NZ, width, PLANE)

    @pl.when(at_ref[0] == 0)
    def _():
        run(1)

    @pl.when(at_ref[0] == 1)
    def _():
        run(-1)


def call(kernel, outs, scratch, name, cost, *args):
    vmem = pl.BlockSpec(memory_space=pltpu.VMEM)
    return pl.pallas_call(
        kernel,
        out_shape=tuple(jax.ShapeDtypeStruct(s, t) for s, t in outs),
        in_specs=[pl.BlockSpec(memory_space=pltpu.SMEM)] + [vmem] * (len(args) - 1),
        out_specs=tuple([vmem] * len(outs)),
        scratch_shapes=[pltpu.VMEM(s, t) for s, t in scratch],
        compiler_params=PARAMS,
        cost_estimate=pl.CostEstimate(flops=cost, bytes_accessed=0, transcendentals=0),
        name=name,
    )(*args)


def swap(values):
    return lax.ppermute(values, "spatial", [(0, 1), (1, 0)])


def around(values, axis, step):
    size = lax.axis_size(axis)
    return lax.ppermute(values, axis, [((i + step) % size, i) for i in range(size)])


def body(features, conv_one, conv_two, cotangent):
    width, channels = conv_one.shape[1], conv_one.shape[2]
    core = lax.axis_index("spatial")
    first = core == 0
    at = jnp.stack([core, lax.axis_index("x"), lax.axis_index("samples")]).astype(jnp.int32)
    one = conv_one.reshape(27 * width, channels)
    two = conv_two.reshape(27 * width, channels)
    features = features.reshape(width, PLANE)
    cotangent = cotangent.reshape(width, PLANE)
    taps = 27 * width
    group = NZ * width
    quarter = channels // 4
    plane = (2, width, PLANE)
    work = 4 * 18 * width * channels * PLANE

    groups = call(regroup_kernel, [((taps, group), BF16)] * NX, [], "regroup", 2 * taps * channels * channels, at, one, two)
    kernels = [groups[0]] + [around(groups[NX - k], "x", k) for k in range(1, NX)]

    came = swap(jnp.where(first, cotangent, features))
    kept = jnp.where(first, features, cotangent)
    block = jnp.where(first, jnp.stack([kept, came]), jnp.stack([came, kept]))
    block, _ = lax.optimization_barrier((block, groups[0]))
    mine = lax.all_to_all(jnp.broadcast_to(block, (NZ,) + block.shape), "z", 0, 0, tiled=True)

    own, *sends, held = call(
        first_kernel,
        [(plane, F32)] + [(plane, BF16)] * (NX - 1) + [((NX, taps, group), BF16)],
        [((NX * 9 * width, 2 * group), BF16), ((2 * group, PLANE), BF16), ((NX * 9 * width, PLANE), F32)],
        "conv_in", work, at, mine, *kernels,
    )
    sends = [around(part, "x", NX - k) for k, part in enumerate(sends, 1)]
    own = own + sum(part.astype(F32) for part in sends)

    left = around(mine, "x", -1)
    right = around(mine, "x", 1)
    far0 = around(left[: NZ // 2], "x", -1)
    far1 = around(right[NZ // 2 :], "x", 1)
    held = swap(held)

    other = swap(own)
    send, keep = call(act_kernel, [(plane, BF16)] * 2, [], "act", 0, at, own, other)
    acts = [send] + [around(send, "x", k) for k in range(1, NX)]
    (parts,) = call(
        second_kernel,
        [((NZ,) + plane, BF16)],
        [((NX * 18 * width, PLANE), BF16), ((NX * 18 * width, group), BF16)],
        "conv_out", work, at, *acts, held,
    )
    parts = lax.all_to_all(parts, "z", 0, 0, tiled=True)

    grads = call(
        grad_kernel,
        [((taps, quarter), BF16)] * 4,
        [((2, channels, PLANE), BF16), ((18 * width, PLANE), BF16), ((taps, channels), BF16)],
        "grad", work, at, keep, mine, left, right, far0, far1,
    )
    pieces = [grads[0]] + [around(grads[4 - k], "samples", k) for k in (1, 2, 3)]
    summed = sum(g.astype(F32) for g in pieces).astype(BF16)
    pieces = [summed] + [around(summed, "samples", k) for k in (1, 2, 3)]
    others = swap(jnp.stack(pieces))
    grad_one, grad_two = call(
        finish_kernel, [((taps, channels), F32)] * 2, [], "finish", 0, at, *pieces, others
    )

    result = jnp.sum(parts.astype(F32), axis=0).astype(BF16)
    ours = jnp.where(first, result[0], result[1])
    theirs = swap(jnp.where(first, result[1], result[0]))
    shape = (width, 1, 1, PLANE)
    mixed_out = jnp.where(first, ours, theirs).reshape(shape)
    input_grad = jnp.where(first, theirs, ours).reshape(shape)
    weights = (27, width, channels)
    return mixed_out, input_grad, grad_one.reshape(weights), grad_two.reshape(weights)


def solution(mesh):
    fine = Mesh(
        mesh.devices.reshape(mesh.shape["samples"], NZ, NX, mesh.shape["spatial"]),
        ("samples", "z", "x", "spatial"),
    )
    acts = P(("z", "x"), "samples", "spatial", None)
    kernels = P(None, ("z", "x"), None)
    return jax.shard_map(
        body,
        mesh=fine,
        in_specs=(acts, kernels, kernels, acts),
        out_specs=(acts, acts, kernels, kernels),
        check_vma=False,
    )
```

```python
import jax
import jax.numpy as jnp
from jax import lax
from jax.experimental import pallas as pl
from jax.experimental.pallas import tpu as pltpu
from jax.sharding import Mesh, PartitionSpec as P

SIDE = 32
PLANE = SIDE * SIDE
F32 = jnp.float32
BF16 = jnp.bfloat16
PARAMS = pltpu.CompilerParams(vmem_limit_bytes=40 * 1024 * 1024)
NX = 4
NZ = 8


def masks(rows):
    cell = lax.broadcasted_iota(jnp.int32, (rows, PLANE), 1)
    column = cell & (SIDE - 1)
    row_ok = {-1: cell >= SIDE, 1: cell < PLANE - SIDE}
    col_ok = {-1: column > 0, 1: column < SIDE - 1}
    return row_ok, col_ok


def moved(values, step, ok):
    return jnp.where(ok, pltpu.roll(values, (-step) % PLANE, 1), 0.0)


def dot(lhs, rhs, dims):
    return lax.dot_general(lhs, rhs, (dims, ((), ())), preferred_element_type=F32)


def tap_sum(stack_ref, start, width, sign, ok):
    row_ok, col_ok = ok
    total = None
    for c in range(3):
        part = None
        for b in range(3):
            at = start + (3 * b + c) * width
            term = stack_ref[at : at + width, :]
            drow = sign * (b - 1)
            if drow:
                term = moved(term, SIDE * drow, row_ok[drow])
            part = term if part is None else part + term
        dcol = sign * (c - 1)
        if dcol:
            part = moved(part, dcol, col_ok[dcol])
        total = part if total is None else total + part
    return total


def spread(values, sign, col_ref, start, ok):
    row_ok, col_ok = ok
    width = values.shape[0]
    for c in range(3):
        dcol = sign * (c - 1)
        part = moved(values, dcol, col_ok[dcol]) if dcol else values
        for b in range(3):
            drow = sign * (b - 1)
            term = moved(part, SIDE * drow, row_ok[drow]) if drow else part
            at = start + (3 * b + c) * width
            col_ref[at : at + width, :] = term.astype(BF16)


def regroup_kernel(at_ref, one_ref, two_ref, *out_refs):
    channels = one_ref.shape[1]
    width = channels // (NX * NZ)
    group = NZ * width
    old = lax.broadcasted_iota(jnp.int32, (channels, group), 0)
    new = lax.broadcasted_iota(jnp.int32, (channels, group), 1)

    def run(ref):
        for k in range(NX):
            x = lax.rem(at_ref[1] + k, NX)
            home = (new // width) * (NX * width) + x * width + new % width
            order = (old == home).astype(F32).astype(BF16)
            out_refs[k][...] = dot(ref[...], order, ((1,), (0,))).astype(BF16)

    @pl.when(at_ref[0] == 0)
    def _():
        run(two_ref)

    @pl.when(at_ref[0] == 1)
    def _():
        run(one_ref)


def first_kernel(at_ref, mine_ref, left_ref, right_ref, far0_ref, far1_ref, one_ref, two_ref, out_ref, whole_ref, near, far):
    width = mine_ref.shape[2]
    third = 9 * width
    ok = masks(width)
    x = at_ref[1]
    half = NZ // 2
    pieces = ((mine_ref, 0, 0, NZ), (left_ref, NX - 1, 0, NZ), (right_ref, 1, 0, NZ), (far0_ref, 2, 0, half), (far1_ref, 2, half, half))
    for ref, step, z0, count in pieces:
        source = lax.rem(x + step, NX)
        for z in range(count):
            rows = pl.ds(pl.multiple_of(((z0 + z) * NX + source) * width, 16), width)
            for d in range(2):
                whole_ref[d, rows, :] = ref[z, d]

    def run(weights, sign):
        low, high = weights[0 : 2 * third, :], weights[third : 3 * third, :]
        first, second = (low, high) if sign > 0 else (high, low)
        near[...] = dot(first, whole_ref[0], ((1,), (0,)))
        far[...] = dot(second, whole_ref[1], ((1,), (0,)))
        near[...] = near[...] + far[...]
        for d in range(2):
            start = third * ((1 - d) if sign > 0 else d)
            out_ref[d] = tap_sum(near, start, width, sign, ok)

    @pl.when(at_ref[0] == 0)
    def _():
        run(one_ref, 1)

    @pl.when(at_ref[0] == 1)
    def _():
        run(two_ref, -1)


def act_kernel(at_ref, own_ref, other_ref, send_ref, keep_ref):
    first = at_ref[0] == 0
    for d in range(2):
        own, other = own_ref[d], other_ref[d]
        pre = jnp.where(first, own, other)
        upstream = jnp.where(first, other, own)
        gate = 1.0 / (1.0 + jnp.exp(-pre))
        hidden = pre * gate
        act = upstream * gate * (1.0 + pre * (1.0 - gate))
        send_ref[d] = jnp.where(first, hidden, act).astype(BF16)
        keep_ref[d] = jnp.where(first, act, hidden).astype(BF16)


def grad_kernel(at_ref, keep_ref, whole_ref, *refs):
    out_refs, (col, full) = refs[:4], refs[4:]
    width = keep_ref.shape[1]
    third = 9 * width
    ok = masks(width)

    def run(sign):
        for d in range(2):
            at = third * (d if sign > 0 else 1 - d)
            spread(keep_ref[d].astype(F32), sign, col, at, ok)
        zero = dot(col[...], whole_ref[0], ((1,), (1,)))
        last = dot(col[...], whole_ref[1], ((1,), (1,)))
        low, high = (last, zero) if sign > 0 else (zero, last)
        full[0:third, :] = low[0:third].astype(BF16)
        full[third : 2 * third, :] = (low[third:] + high[0:third]).astype(BF16)
        full[2 * third :, :] = high[third:].astype(BF16)

    @pl.when(at_ref[0] == 0)
    def _():
        run(-1)

    @pl.when(at_ref[0] == 1)
    def _():
        run(1)

    quarter = full.shape[1] // 4
    for k in range(4):
        columns = pl.ds(pl.multiple_of(lax.rem(at_ref[2] + k, 4) * quarter, quarter), quarter)
        out_refs[k][...] = full[:, columns]


def finish_kernel(at_ref, *refs):
    own_refs, other_ref, (one_ref, two_ref) = refs[:4], refs[4], refs[5:]
    quarter = other_ref.shape[2]

    def run(own_out, other_out):
        for k in range(4):
            columns = pl.ds(pl.multiple_of(lax.rem(at_ref[2] + k, 4) * quarter, quarter), quarter)
            own_out[:, columns] = own_refs[k][...].astype(F32)
            other_out[:, columns] = other_ref[k].astype(F32)

    @pl.when(at_ref[0] == 0)
    def _():
        run(one_ref, two_ref)

    @pl.when(at_ref[0] == 1)
    def _():
        run(two_ref, one_ref)


def second_kernel(at_ref, *refs):
    acts, kernels, (out_ref, col, tall) = refs[:NX], refs[NX : 2 * NX], refs[2 * NX :]
    width = acts[0].shape[1]
    third = 9 * width
    ok = masks(width)

    def run(sign):
        for k in range(NX):
            for d in range(2):
                at = 2 * third * k + third * (d if sign > 0 else 1 - d)
                spread(acts[k][d].astype(F32), sign, col, at, ok)
        for d in range(2):
            at = third * ((1 - d) if sign > 0 else d)
            for k in range(NX):
                tall[2 * third * k : 2 * third * (k + 1), :] = kernels[k][at : at + 2 * third, :]
            part = dot(tall[...], col[...], ((0,), (0,)))
            out_ref[:, d] = part.astype(BF16).reshape(NZ, width, PLANE)

    @pl.when(at_ref[0] == 0)
    def _():
        run(1)

    @pl.when(at_ref[0] == 1)
    def _():
        run(-1)


def call(kernel, outs, scratch, name, cost, *args):
    vmem = pl.BlockSpec(memory_space=pltpu.VMEM)
    return pl.pallas_call(
        kernel,
        out_shape=tuple(jax.ShapeDtypeStruct(s, t) for s, t in outs),
        in_specs=[pl.BlockSpec(memory_space=pltpu.SMEM)] + [vmem] * (len(args) - 1),
        out_specs=tuple([vmem] * len(outs)),
        scratch_shapes=[pltpu.VMEM(s, t) for s, t in scratch],
        compiler_params=PARAMS,
        cost_estimate=pl.CostEstimate(flops=cost, bytes_accessed=0, transcendentals=0),
        name=name,
    )(*args)


def swap(values):
    return lax.ppermute(values, "spatial", [(0, 1), (1, 0)])


def around(values, axis, step):
    size = lax.axis_size(axis)
    return lax.ppermute(values, axis, [((i + step) % size, i) for i in range(size)])


def body(features, conv_one, conv_two, cotangent):
    width, channels = conv_one.shape[1], conv_one.shape[2]
    at = jnp.stack([lax.axis_index(a) for a in ("spatial", "x", "samples")]).astype(jnp.int32)
    one = conv_one.reshape(27 * width, channels)
    two = conv_two.reshape(27 * width, channels)
    taps = 27 * width
    group = NZ * width
    quarter = channels // 4
    plane = (2, width, PLANE)
    everyone = (2 * NZ, width, PLANE)
    work = 4 * 18 * width * channels * PLANE

    pair = jnp.stack([features.reshape(width, PLANE), cotangent.reshape(width, PLANE)])
    pair = jnp.broadcast_to(pair, (NZ,) + plane).reshape(everyone)
    mine = lax.all_to_all(pair, ("z", "spatial"), 0, 0, tiled=True).reshape((NZ,) + plane)

    groups = call(regroup_kernel, [((taps, group), BF16)] * NX, [], "regroup", 2 * taps * channels * channels, at, one, two)
    kernels = [groups[0]] + [around(groups[NX - k], "x", k) for k in range(1, NX)]
    mine, kernels = lax.optimization_barrier((mine, kernels))

    left = around(mine, "x", -1)
    right = around(mine, "x", 1)
    far0 = around(left[: NZ // 2], "x", -1)
    far1 = around(right[NZ // 2 :], "x", 1)

    own, whole = call(
        first_kernel,
        [(plane, F32), ((2, channels, PLANE), BF16)],
        [((18 * width, PLANE), F32)] * 2,
        "conv_in", work, at, mine, left, right, far0, far1, one, two,
    )
    other = swap(own)
    send, keep = call(act_kernel, [(plane, BF16)] * 2, [], "act", 0, at, own, other)
    acts = [send] + [around(send, "x", k) for k in range(1, NX)]
    grads = call(
        grad_kernel,
        [((taps, quarter), BF16)] * 4,
        [((18 * width, PLANE), BF16), ((taps, channels), BF16)],
        "grad", work, at, keep, whole,
    )
    (parts,) = call(
        second_kernel,
        [((NZ,) + plane, BF16)],
        [((NX * 18 * width, PLANE), BF16), ((NX * 18 * width, group), BF16)],
        "conv_out", work, at, *acts, *kernels,
    )
    parts = lax.all_to_all(parts.reshape(everyone), ("z", "spatial"), 0, 0, tiled=True)

    pieces = [grads[0]] + [around(grads[4 - k], "samples", k) for k in (1, 2, 3)]
    summed = sum(g.astype(F32) for g in pieces).astype(BF16)
    pieces = [summed] + [around(summed, "samples", k) for k in (1, 2, 3)]
    others = swap(jnp.stack(pieces))
    grad_one, grad_two = call(
        finish_kernel, [((taps, channels), F32)] * 2, [], "finish", 0, at, *pieces, others
    )
    parts, grad_one, grad_two = lax.optimization_barrier((parts, grad_one, grad_two))

    result = jnp.sum(parts.reshape((NZ,) + plane).astype(F32), axis=0).astype(BF16)
    shape = (width, 1, 1, PLANE)
    weights = (27, width, channels)
    return result[0].reshape(shape), result[1].reshape(shape), grad_one.reshape(weights), grad_two.reshape(weights)


def solution(mesh):
    fine = Mesh(
        mesh.devices.reshape(mesh.shape["samples"], NZ, NX, mesh.shape["spatial"]),
        ("samples", "z", "x", "spatial"),
    )
    acts = P(("z", "x"), "samples", "spatial", None)
    kernels = P(None, ("z", "x"), None)
    return jax.shard_map(
        body,
        mesh=fine,
        in_specs=(acts, kernels, kernels, acts),
        out_specs=(acts, acts, kernels, kernels),
        check_vma=False,
    )
```

```python
import jax
import jax.numpy as jnp
from jax import lax
from jax.experimental import pallas as pl
from jax.experimental.pallas import tpu as pltpu
from jax.sharding import Mesh, PartitionSpec as P

SIDE = 32
PLANE = SIDE * SIDE
F32 = jnp.float32
BF16 = jnp.bfloat16
PARAMS = pltpu.CompilerParams(vmem_limit_bytes=40 * 1024 * 1024)
NX = 4
NZ = 8


def masks(rows):
    cell = lax.broadcasted_iota(jnp.int32, (rows, PLANE), 1)
    column = cell & (SIDE - 1)
    row_ok = {-1: cell >= SIDE, 1: cell < PLANE - SIDE}
    col_ok = {-1: column > 0, 1: column < SIDE - 1}
    return row_ok, col_ok


def moved(values, step, ok):
    return jnp.where(ok, pltpu.roll(values, (-step) % PLANE, 1), 0.0)


def dot(lhs, rhs, dims):
    return lax.dot_general(lhs, rhs, (dims, ((), ())), preferred_element_type=F32)


def tap_sum(stack_ref, start, width, sign, ok):
    row_ok, col_ok = ok
    total = None
    for c in range(3):
        part = None
        for b in range(3):
            at = start + (3 * b + c) * width
            term = stack_ref[at : at + width, :]
            drow = sign * (b - 1)
            if drow:
                term = moved(term, SIDE * drow, row_ok[drow])
            part = term if part is None else part + term
        dcol = sign * (c - 1)
        if dcol:
            part = moved(part, dcol, col_ok[dcol])
        total = part if total is None else total + part
    return total


def spread(values, sign, col_ref, start, ok):
    row_ok, col_ok = ok
    width = values.shape[0]
    for c in range(3):
        dcol = sign * (c - 1)
        part = moved(values, dcol, col_ok[dcol]) if dcol else values
        for b in range(3):
            drow = sign * (b - 1)
            term = moved(part, SIDE * drow, row_ok[drow]) if drow else part
            at = start + (3 * b + c) * width
            col_ref[at : at + width, :] = term.astype(BF16)


def regroup_kernel(at_ref, one_ref, two_ref, *out_refs):
    channels = one_ref.shape[1]
    width = channels // (NX * NZ)
    group = NZ * width
    old = lax.broadcasted_iota(jnp.int32, (channels, group), 0)
    new = lax.broadcasted_iota(jnp.int32, (channels, group), 1)

    def run(ref):
        for k in range(NX):
            x = lax.rem(at_ref[1] + k, NX)
            home = (new // width) * (NX * width) + x * width + new % width
            order = (old == home).astype(F32).astype(BF16)
            out_refs[k][...] = dot(ref[...], order, ((1,), (0,))).astype(BF16)

    @pl.when(at_ref[0] == 0)
    def _():
        run(one_ref)

    @pl.when(at_ref[0] == 1)
    def _():
        run(two_ref)


def first_kernel(at_ref, mine_ref, *refs):
    kernels, own_ref, out_refs = refs[:NX], refs[NX], refs[NX + 1 : 2 * NX]
    all_ref, lhs, rhs, stack = refs[2 * NX :]
    width = mine_ref.shape[2]
    group = NZ * width
    third = 9 * width
    ok = masks(width)
    for d in range(2):
        rhs[d * group : (d + 1) * group, :] = mine_ref[:, d].reshape(group, PLANE)
    for k in range(NX):
        all_ref[k] = kernels[k][...]

    def run(sign):
        for d in range(2):
            for k in range(NX):
                for e in range(2):
                    a = 1 + sign * (e - d)
                    lhs[k * third : (k + 1) * third, e * group : (e + 1) * group] = kernels[k][a * third : (a + 1) * third, :]
            stack[...] = dot(lhs[...], rhs[...], ((1,), (0,)))
            for k in range(NX):
                total = tap_sum(stack, k * third, width, sign, ok)
                if k:
                    out_refs[k - 1][d] = total.astype(BF16)
                else:
                    own_ref[d] = total

    @pl.when(at_ref[0] == 0)
    def _():
        run(1)

    @pl.when(at_ref[0] == 1)
    def _():
        run(-1)


def act_kernel(at_ref, own_ref, other_ref, send_ref):
    first = at_ref[0] == 0
    for d in range(2):
        own, other = own_ref[d], other_ref[d]
        pre = jnp.where(first, own, other)
        upstream = jnp.where(first, other, own)
        gate = 1.0 / (1.0 + jnp.exp(-pre))
        hidden = pre * gate
        act = upstream * gate * (1.0 + pre * (1.0 - gate))
        send_ref[d] = jnp.where(first, hidden, act).astype(BF16)


def second_kernel(at_ref, *refs):
    acts, held, across, (out_ref, grad_ref, col, tall, both) = refs[:NX], refs[NX], refs[NX + 1], refs[NX + 2 :]
    width = held.shape[1] // 27
    third = 9 * width
    group = NZ * width
    ok = masks(width)

    def run(sign):
        for k in range(NX):
            for d in range(2):
                at = 2 * third * k + third * (d if sign > 0 else 1 - d)
                spread(acts[k][d].astype(F32), sign, col, at, ok)
        for d in range(2):
            both[d * group : (d + 1) * group, :] = across[:, d].reshape(group, PLANE)
        grad = dot(col[...], both[...], ((1,), (1,)))
        zero, last = grad[:, 0:group], grad[:, group:]
        low, high = (last, zero) if sign > 0 else (zero, last)
        for k in range(NX):
            at, mid, end = (2 * k + 0) * third, (2 * k + 1) * third, (2 * k + 2) * third
            taps = jnp.concatenate([low[at:mid], low[mid:end] + high[at:mid], high[mid:end]], axis=0).astype(BF16)
            x = lax.rem(at_ref[1] + k, NX)
            size = grad_ref.shape[1]
            for y in range(4):
                rows = taps[y * size : min((y + 1) * size, 3 * third)]
                grad_ref[y * NX + x, 0 : rows.shape[0], :] = rows
                if rows.shape[0] < size:
                    grad_ref[y * NX + x, rows.shape[0] :, :] = jnp.zeros((size - rows.shape[0], group), BF16)
        for d in range(2):
            at = third * ((1 - d) if sign > 0 else d)
            for k in range(NX):
                tall[2 * third * k : 2 * third * (k + 1), :] = held[k, at : at + 2 * third, :]
            part = dot(tall[...], col[...], ((0,), (0,)))
            out_ref[:, d] = part.astype(BF16).reshape(NZ, width, PLANE)

    @pl.when(at_ref[0] == 0)
    def _():
        run(1)

    @pl.when(at_ref[0] == 1)
    def _():
        run(-1)


def finish_kernel(at_ref, *refs):
    own_refs, other_ref, (one_ref, two_ref, near, far) = refs[:4], refs[4], refs[5:]
    taps, channels = one_ref.shape
    _, _, size, group = other_ref.shape
    width = group // NZ
    old = lax.broadcasted_iota(jnp.int32, (channels, channels), 0)
    new = lax.broadcasted_iota(jnp.int32, (channels, channels), 1)
    place = (new // width) % NX * group + new // (NX * width) * width + new % width
    order = (old == place).astype(F32).astype(BF16)

    def put(piece, full, out_ref):
        for k in range(4):
            rows = pl.ds(pl.multiple_of(lax.rem(at_ref[2] + k, 4) * size, 16), size)
            for x in range(NX):
                full[rows, x * group : (x + 1) * group] = piece(k, x)
        out_ref[...] = dot(full[0:taps, :], order, ((1,), (0,)))

    def run(own_out, other_out):
        put(lambda k, x: own_refs[k][x], near, own_out)
        put(lambda k, x: other_ref[k, x], far, other_out)

    @pl.when(at_ref[0] == 0)
    def _():
        run(two_ref, one_ref)

    @pl.when(at_ref[0] == 1)
    def _():
        run(one_ref, two_ref)


def call(kernel, outs, scratch, name, cost, *args):
    vmem = pl.BlockSpec(memory_space=pltpu.VMEM)
    return pl.pallas_call(
        kernel,
        out_shape=tuple(jax.ShapeDtypeStruct(s, t) for s, t in outs),
        in_specs=[pl.BlockSpec(memory_space=pltpu.SMEM)] + [vmem] * (len(args) - 1),
        out_specs=tuple([vmem] * len(outs)),
        scratch_shapes=[pltpu.VMEM(s, t) for s, t in scratch],
        compiler_params=PARAMS,
        cost_estimate=pl.CostEstimate(flops=cost, bytes_accessed=0, transcendentals=0),
        name=name,
    )(*args)


def swap(values):
    return lax.ppermute(values, "spatial", [(0, 1), (1, 0)])


def around(values, axis, step):
    size = lax.axis_size(axis)
    return lax.ppermute(values, axis, [((i + step) % size, i) for i in range(size)])


def body(features, conv_one, conv_two, cotangent):
    width, channels = conv_one.shape[1], conv_one.shape[2]
    at = jnp.stack([lax.axis_index(a) for a in ("spatial", "x", "samples")]).astype(jnp.int32)
    one = conv_one.reshape(27 * width, channels)
    two = conv_two.reshape(27 * width, channels)
    taps = 27 * width
    group = NZ * width
    plane = (2, width, PLANE)
    everyone = (2 * NZ, width, PLANE)
    piece = (7 * width, group)
    work = 4 * 18 * width * channels * PLANE

    pair = jnp.stack([features.reshape(width, PLANE), cotangent.reshape(width, PLANE)])
    pair = jnp.broadcast_to(pair, (NZ,) + plane).reshape(everyone)
    mine = lax.all_to_all(pair, ("z", "spatial"), 0, 0, tiled=True).reshape((NZ,) + plane)

    groups = call(regroup_kernel, [((taps, group), BF16)] * NX, [], "regroup", 2 * taps * channels * channels, at, one, two)
    kernels = [groups[0]] + [around(groups[NX - k], "x", k) for k in range(1, NX)]

    own, *sends, held = call(
        first_kernel,
        [(plane, F32)] + [(plane, BF16)] * (NX - 1) + [((NX, taps, group), BF16)],
        [((NX * 9 * width, 2 * group), BF16), ((2 * group, PLANE), BF16), ((NX * 9 * width, PLANE), F32)],
        "conv_in", work, at, mine, *kernels,
    )
    sends = [around(part, "x", NX - k) for k, part in enumerate(sends, 1)]
    own = own + sum(part.astype(F32) for part in sends)
    held, across = swap(held), swap(mine)

    (send,) = call(act_kernel, [(plane, BF16)], [], "act", 0, at, own, swap(own))
    acts = [send] + [around(send, "x", k) for k in range(1, NX)]
    parts, grads = call(
        second_kernel,
        [((NZ,) + plane, BF16), ((4 * NX,) + piece, BF16)],
        [((NX * 18 * width, PLANE), BF16), ((NX * 18 * width, group), BF16), ((2 * group, PLANE), BF16)],
        "conv_out", 2 * work, at, *acts, held, across,
    )
    grads = lax.all_to_all(grads, ("samples", "x"), 0, 0, tiled=True)
    parts = lax.all_to_all(parts.reshape(everyone), ("z", "spatial"), 0, 0, tiled=True)

    summed = jnp.sum(grads.reshape((4, NX) + piece).astype(F32), axis=0).astype(BF16)
    pieces = [summed] + [around(summed, "samples", k) for k in (1, 2, 3)]
    others = swap(jnp.stack(pieces))
    grad_one, grad_two = call(
        finish_kernel, [((taps, channels), F32)] * 2, [((28 * width, channels), BF16)] * 2, "finish", 0, at, *pieces, others
    )
    parts, grad_one, grad_two = lax.optimization_barrier((parts, grad_one, grad_two))

    result = jnp.sum(parts.reshape((NZ,) + plane).astype(F32), axis=0).astype(BF16)
    shape = (width, 1, 1, PLANE)
    weights = (27, width, channels)
    return result[0].reshape(shape), result[1].reshape(shape), grad_one.reshape(weights), grad_two.reshape(weights)


def solution(mesh):
    fine = Mesh(
        mesh.devices.reshape(mesh.shape["samples"], NZ, NX, mesh.shape["spatial"]),
        ("samples", "z", "x", "spatial"),
    )
    acts = P(("z", "x"), "samples", "spatial", None)
    kernels = P(None, ("z", "x"), None)
    return jax.shard_map(
        body,
        mesh=fine,
        in_specs=(acts, kernels, kernels, acts),
        out_specs=(acts, acts, kernels, kernels),
        check_vma=False,
    )
```

```python
import jax
import jax.numpy as jnp
from jax import lax
from jax.experimental import pallas as pl
from jax.experimental.pallas import tpu as pltpu
from jax.sharding import Mesh, PartitionSpec as P

SIDE = 32
PLANE = SIDE * SIDE
F32 = jnp.float32
BF16 = jnp.bfloat16
PARAMS = pltpu.CompilerParams(vmem_limit_bytes=40 * 1024 * 1024)
NX = 4
NZ = 8


def masks(rows):
    cell = lax.broadcasted_iota(jnp.int32, (rows, PLANE), 1)
    column = cell & (SIDE - 1)
    row_ok = {-1: cell >= SIDE, 1: cell < PLANE - SIDE}
    col_ok = {-1: column > 0, 1: column < SIDE - 1}
    return row_ok, col_ok


def moved(values, step, ok):
    return jnp.where(ok, pltpu.roll(values, (-step) % PLANE, 1), 0.0)


def dot(lhs, rhs, dims):
    return lax.dot_general(lhs, rhs, (dims, ((), ())), preferred_element_type=F32)


def tap_sum(stack_ref, start, width, sign, ok):
    row_ok, col_ok = ok
    total = None
    for c in range(3):
        part = None
        for b in range(3):
            at = start + (3 * b + c) * width
            term = stack_ref[at : at + width, :]
            drow = sign * (b - 1)
            if drow:
                term = moved(term, SIDE * drow, row_ok[drow])
            part = term if part is None else part + term
        dcol = sign * (c - 1)
        if dcol:
            part = moved(part, dcol, col_ok[dcol])
        total = part if total is None else total + part
    return total


def spread(values, sign, col_ref, start, ok):
    row_ok, col_ok = ok
    width = values.shape[0]
    for c in range(3):
        dcol = sign * (c - 1)
        part = moved(values, dcol, col_ok[dcol]) if dcol else values
        for b in range(3):
            drow = sign * (b - 1)
            term = moved(part, SIDE * drow, row_ok[drow]) if drow else part
            at = start + (3 * b + c) * width
            col_ref[at : at + width, :] = term.astype(BF16)


def regroup_kernel(at_ref, one_ref, two_ref, *out_refs):
    channels = one_ref.shape[1]
    width = channels // (NX * NZ)
    group = NZ * width
    old = lax.broadcasted_iota(jnp.int32, (channels, group), 0)
    new = lax.broadcasted_iota(jnp.int32, (channels, group), 1)

    def run(ref):
        for k in range(NX):
            x = lax.rem(at_ref[1] + k, NX)
            home = (new // width) * (NX * width) + x * width + new % width
            order = (old == home).astype(F32).astype(BF16)
            out_refs[k][...] = dot(ref[...], order, ((1,), (0,))).astype(BF16)

    @pl.when(at_ref[0] == 0)
    def _():
        run(one_ref)

    @pl.when(at_ref[0] == 1)
    def _():
        run(two_ref)


def first_kernel(at_ref, mine_ref, *refs):
    kernels, own_ref, out_refs = refs[:NX], refs[NX], refs[NX + 1 : 2 * NX]
    all_ref, lhs, rhs, stack = refs[2 * NX :]
    width = mine_ref.shape[2]
    group = NZ * width
    third = 9 * width
    ok = masks(width)
    for d in range(2):
        rhs[d * group : (d + 1) * group, :] = mine_ref[:, d].reshape(group, PLANE)
    for k in range(NX):
        all_ref[k] = kernels[k][...]

    def run(sign):
        for d in range(2):
            for k in range(NX):
                for e in range(2):
                    a = 1 + sign * (e - d)
                    lhs[k * third : (k + 1) * third, e * group : (e + 1) * group] = kernels[k][a * third : (a + 1) * third, :]
            stack[...] = dot(lhs[...], rhs[...], ((1,), (0,)))
            for k in range(NX):
                total = tap_sum(stack, k * third, width, sign, ok)
                if k:
                    out_refs[k - 1][d] = total.astype(BF16)
                else:
                    own_ref[d] = total

    @pl.when(at_ref[0] == 0)
    def _():
        run(1)

    @pl.when(at_ref[0] == 1)
    def _():
        run(-1)


def act_kernel(at_ref, own_ref, other_ref, send_ref):
    first = at_ref[0] == 0
    for d in range(2):
        own, other = own_ref[d], other_ref[d]
        pre = jnp.where(first, own, other)
        upstream = jnp.where(first, other, own)
        gate = 1.0 / (1.0 + jnp.exp(-pre))
        hidden = pre * gate
        act = upstream * gate * (1.0 + pre * (1.0 - gate))
        send_ref[d] = jnp.where(first, hidden, act).astype(BF16)


def grad_kernel(at_ref, *refs):
    acts, across, (grad_ref, col, both) = refs[:NX], refs[NX], refs[NX + 1 :]
    width = acts[0].shape[1]
    third = 9 * width
    group = NZ * width
    ok = masks(width)

    def run(sign):
        for k in range(NX):
            for d in range(2):
                at = 2 * third * k + third * (d if sign > 0 else 1 - d)
                spread(acts[k][d].astype(F32), sign, col, at, ok)
        for d in range(2):
            both[d * group : (d + 1) * group, :] = across[:, d].reshape(group, PLANE)
        grad = dot(col[...], both[...], ((1,), (1,)))
        zero, last = grad[:, 0:group], grad[:, group:]
        low, high = (last, zero) if sign > 0 else (zero, last)
        for k in range(NX):
            at, mid, end = (2 * k + 0) * third, (2 * k + 1) * third, (2 * k + 2) * third
            taps = jnp.concatenate([low[at:mid], low[mid:end] + high[at:mid], high[mid:end]], axis=0).astype(BF16)
            x = lax.rem(at_ref[1] + k, NX)
            size = grad_ref.shape[1]
            for y in range(4):
                rows = taps[y * size : min((y + 1) * size, 3 * third)]
                grad_ref[y * NX + x, 0 : rows.shape[0], :] = rows
                if rows.shape[0] < size:
                    grad_ref[y * NX + x, rows.shape[0] :, :] = jnp.zeros((size - rows.shape[0], group), BF16)

    @pl.when(at_ref[0] == 0)
    def _():
        run(1)

    @pl.when(at_ref[0] == 1)
    def _():
        run(-1)


def second_kernel(at_ref, col, held, out_ref, tall):
    width = held.shape[1] // 27
    third = 9 * width
    for d in range(2):
        at = pl.multiple_of(third * jnp.where(at_ref[0] == 0, 1 - d, d), 16)
        for k in range(NX):
            tall[d, 2 * third * k : 2 * third * (k + 1), :] = held[k, pl.ds(at, 2 * third), :]
        part = dot(tall[d], col[...], ((0,), (0,)))
        out_ref[:, d] = part.astype(BF16).reshape(NZ, width, PLANE)


def pack_kernel(at_ref, features_ref, cotangent_ref, out_ref):
    for z in range(NZ):
        out_ref[z, 0] = features_ref[...]
        out_ref[z, 1] = cotangent_ref[...]


def sum_kernel(at_ref, parts_ref, mixed_ref, input_ref):
    for d, out_ref in enumerate((mixed_ref, input_ref)):
        total = parts_ref[0, d].astype(F32)
        for z in range(1, NZ):
            total = total + parts_ref[z, d].astype(F32)
        out_ref[...] = total.astype(BF16)


def finish_kernel(at_ref, *refs):
    own_refs, other_ref, (one_ref, two_ref, near, far) = refs[:4], refs[4], refs[5:]
    taps, channels = one_ref.shape
    _, _, size, group = other_ref.shape
    width = group // NZ
    old = lax.broadcasted_iota(jnp.int32, (channels, channels), 0)
    new = lax.broadcasted_iota(jnp.int32, (channels, channels), 1)
    place = (new // width) % NX * group + new // (NX * width) * width + new % width
    order = (old == place).astype(F32).astype(BF16)

    def put(piece, full, out_ref):
        for k in range(4):
            rows = pl.ds(pl.multiple_of(lax.rem(at_ref[2] + k, 4) * size, 16), size)
            for x in range(NX):
                full[rows, x * group : (x + 1) * group] = piece(k, x)
        out_ref[...] = dot(full[0:taps, :], order, ((1,), (0,)))

    def run(own_out, other_out):
        put(lambda k, x: own_refs[k][x], near, own_out)
        put(lambda k, x: other_ref[k, x], far, other_out)

    @pl.when(at_ref[0] == 0)
    def _():
        run(two_ref, one_ref)

    @pl.when(at_ref[0] == 1)
    def _():
        run(one_ref, two_ref)


def call(kernel, outs, scratch, name, cost, *args):
    vmem = pl.BlockSpec(memory_space=pltpu.VMEM)
    return pl.pallas_call(
        kernel,
        out_shape=tuple(jax.ShapeDtypeStruct(s, t) for s, t in outs),
        in_specs=[pl.BlockSpec(memory_space=pltpu.SMEM)] + [vmem] * (len(args) - 1),
        out_specs=tuple([vmem] * len(outs)),
        scratch_shapes=[pltpu.VMEM(s, t) for s, t in scratch],
        compiler_params=PARAMS,
        cost_estimate=pl.CostEstimate(flops=cost, bytes_accessed=0, transcendentals=0),
        name=name,
    )(*args)


def swap(values):
    return lax.ppermute(values, "spatial", [(0, 1), (1, 0)])


def around(values, axis, step):
    size = lax.axis_size(axis)
    return lax.ppermute(values, axis, [((i + step) % size, i) for i in range(size)])


def body(features, conv_one, conv_two, cotangent):
    width, channels = conv_one.shape[1], conv_one.shape[2]
    at = jnp.stack([lax.axis_index(a) for a in ("spatial", "x", "samples")]).astype(jnp.int32)
    one = conv_one.reshape(27 * width, channels)
    two = conv_two.reshape(27 * width, channels)
    taps = 27 * width
    group = NZ * width
    plane = (2, width, PLANE)
    everyone = (2 * NZ, width, PLANE)
    piece = (7 * width, group)
    work = 4 * 18 * width * channels * PLANE

    (pair,) = call(
        pack_kernel, [((NZ,) + plane, BF16)], [], "pack", 0,
        at, features.reshape(width, PLANE), cotangent.reshape(width, PLANE),
    )
    mine = lax.all_to_all(pair.reshape(everyone), ("z", "spatial"), 0, 0, tiled=True).reshape((NZ,) + plane)

    groups = call(regroup_kernel, [((taps, group), BF16)] * NX, [], "regroup", 2 * taps * channels * channels, at, one, two)
    kernels = [groups[0]] + [around(groups[NX - k], "x", k) for k in range(1, NX)]

    own, *sends, held = call(
        first_kernel,
        [(plane, F32)] + [(plane, BF16)] * (NX - 1) + [((NX, taps, group), BF16)],
        [((NX * 9 * width, 2 * group), BF16), ((2 * group, PLANE), BF16), ((NX * 9 * width, PLANE), F32)],
        "conv_in", work, at, mine, *kernels,
    )
    sends = [around(part, "x", NX - k) for k, part in enumerate(sends, 1)]
    own = own + sum(part.astype(F32) for part in sends)
    held, across = swap(held), swap(mine)

    (send,) = call(act_kernel, [(plane, BF16)], [], "act", 0, at, own, swap(own))
    acts = [send] + [around(send, "x", k) for k in range(1, NX)]
    grads, col = call(
        grad_kernel,
        [((4 * NX,) + piece, BF16), ((NX * 18 * width, PLANE), BF16)],
        [((2 * group, PLANE), BF16)],
        "grad", work, at, *acts, across,
    )
    grads = lax.all_to_all(grads, ("samples", "x"), 0, 0, tiled=True)
    (parts,) = call(
        second_kernel,
        [((NZ,) + plane, BF16)],
        [((2, NX * 18 * width, group), BF16)],
        "conv_out", work, at, col, held,
    )
    parts, grads = lax.optimization_barrier((parts, grads))
    parts = lax.all_to_all(parts.reshape(everyone), ("z", "spatial"), 0, 0, tiled=True)

    summed = jnp.sum(grads.reshape((4, NX) + piece).astype(F32), axis=0).astype(BF16)
    pieces = [summed] + [around(summed, "samples", k) for k in (1, 2, 3)]
    others = swap(jnp.stack(pieces))
    grad_one, grad_two = call(
        finish_kernel, [((taps, channels), F32)] * 2, [((28 * width, channels), BF16)] * 2, "finish", 0, at, *pieces, others
    )
    parts, grad_one, grad_two = lax.optimization_barrier((parts, grad_one, grad_two))

    mixed_out, input_grad = call(
        sum_kernel, [((width, PLANE), BF16)] * 2, [], "sum", 0, at, parts.reshape((NZ,) + plane)
    )
    shape = (width, 1, 1, PLANE)
    weights = (27, width, channels)
    return mixed_out.reshape(shape), input_grad.reshape(shape), grad_one.reshape(weights), grad_two.reshape(weights)


def solution(mesh):
    fine = Mesh(
        mesh.devices.reshape(mesh.shape["samples"], NZ, NX, mesh.shape["spatial"]),
        ("samples", "z", "x", "spatial"),
    )
    acts = P(("z", "x"), "samples", "spatial", None)
    kernels = P(None, ("z", "x"), None)
    return jax.shard_map(
        body,
        mesh=fine,
        in_specs=(acts, kernels, kernels, acts),
        out_specs=(acts, acts, kernels, kernels),
        check_vma=False,
    )
```

```python
import jax
import jax.numpy as jnp
from jax import lax
from jax.experimental import pallas as pl
from jax.experimental.pallas import tpu as pltpu
from jax.sharding import Mesh, PartitionSpec as P

SIDE = 32
PLANE = SIDE * SIDE
F32 = jnp.float32
BF16 = jnp.bfloat16
PARAMS = pltpu.CompilerParams(vmem_limit_bytes=40 * 1024 * 1024)
NX = 4
NZ = 8


def masks(rows):
    cell = lax.broadcasted_iota(jnp.int32, (rows, PLANE), 1)
    column = cell & (SIDE - 1)
    row_ok = {-1: cell >= SIDE, 1: cell < PLANE - SIDE}
    col_ok = {-1: column > 0, 1: column < SIDE - 1}
    return row_ok, col_ok


def moved(values, step, ok):
    return jnp.where(ok, pltpu.roll(values, (-step) % PLANE, 1), 0.0)


def dot(lhs, rhs, dims):
    return lax.dot_general(lhs, rhs, (dims, ((), ())), preferred_element_type=F32)


def tap_sum(stack_ref, start, width, sign, ok):
    row_ok, col_ok = ok
    total = None
    for c in range(3):
        part = None
        for b in range(3):
            at = start + (3 * b + c) * width
            term = stack_ref[at : at + width, :]
            drow = sign * (b - 1)
            if drow:
                term = moved(term, SIDE * drow, row_ok[drow])
            part = term if part is None else part + term
        dcol = sign * (c - 1)
        if dcol:
            part = moved(part, dcol, col_ok[dcol])
        total = part if total is None else total + part
    return total


def spread(values, sign, col_ref, start, ok):
    row_ok, col_ok = ok
    width = values.shape[0]
    for c in range(3):
        dcol = sign * (c - 1)
        part = moved(values, dcol, col_ok[dcol]) if dcol else values
        for b in range(3):
            drow = sign * (b - 1)
            term = moved(part, SIDE * drow, row_ok[drow]) if drow else part
            at = start + (3 * b + c) * width
            col_ref[at : at + width, :] = term.astype(BF16)


def regroup_kernel(at_ref, one_ref, two_ref, *out_refs):
    channels = one_ref.shape[1]
    width = channels // (NX * NZ)
    group = NZ * width
    old = lax.broadcasted_iota(jnp.int32, (channels, group), 0)
    new = lax.broadcasted_iota(jnp.int32, (channels, group), 1)

    def run(ref):
        for k in range(NX):
            x = lax.rem(at_ref[1] + k, NX)
            home = (new // width) * (NX * width) + x * width + new % width
            order = (old == home).astype(F32).astype(BF16)
            out_refs[k][...] = dot(ref[...], order, ((1,), (0,))).astype(BF16)

    @pl.when(at_ref[0] == 0)
    def _():
        run(one_ref)

    @pl.when(at_ref[0] == 1)
    def _():
        run(two_ref)


def first_kernel(at_ref, mine_ref, *refs):
    kernels, own_ref, out_refs = refs[:NX], refs[NX], refs[NX + 1 : 2 * NX]
    all_ref, lhs, rhs, stack = refs[2 * NX :]
    width = mine_ref.shape[2]
    group = NZ * width
    third = 9 * width
    ok = masks(width)
    for d in range(2):
        rhs[d * group : (d + 1) * group, :] = mine_ref[:, d].reshape(group, PLANE)
    for k in range(NX):
        all_ref[k] = kernels[k][...]

    def run(sign):
        for d in range(2):
            for k in range(NX):
                for e in range(2):
                    a = 1 + sign * (e - d)
                    lhs[k * third : (k + 1) * third, e * group : (e + 1) * group] = kernels[k][a * third : (a + 1) * third, :]
            stack[...] = dot(lhs[...], rhs[...], ((1,), (0,)))
            for k in range(NX):
                total = tap_sum(stack, k * third, width, sign, ok)
                if k:
                    out_refs[k - 1][d] = total.astype(BF16)
                else:
                    own_ref[d] = total

    @pl.when(at_ref[0] == 0)
    def _():
        run(1)

    @pl.when(at_ref[0] == 1)
    def _():
        run(-1)


def act_kernel(at_ref, own_ref, other_ref, send_ref):
    first = at_ref[0] == 0
    for d in range(2):
        own, other = own_ref[d], other_ref[d]
        pre = jnp.where(first, own, other)
        upstream = jnp.where(first, other, own)
        gate = 1.0 / (1.0 + jnp.exp(-pre))
        hidden = pre * gate
        act = upstream * gate * (1.0 + pre * (1.0 - gate))
        send_ref[d] = jnp.where(first, hidden, act).astype(BF16)


def second_kernel(at_ref, *refs):
    acts, held, across, refs = refs[:NX], refs[NX], refs[NX + 1], refs[NX + 2 :]
    out_refs, (grad_ref, col, tall, both, parts) = refs[:NZ], refs[NZ:]
    width = held.shape[1] // 27
    third = 9 * width
    group = NZ * width
    ok = masks(width)

    def run(sign):
        for k in range(NX):
            for d in range(2):
                at = 2 * third * k + third * (d if sign > 0 else 1 - d)
                spread(acts[k][d].astype(F32), sign, col, at, ok)
        for d in range(2):
            both[d * group : (d + 1) * group, :] = across[:, d].reshape(group, PLANE)
        grad = dot(col[...], both[...], ((1,), (1,)))
        zero, last = grad[:, 0:group], grad[:, group:]
        low, high = (last, zero) if sign > 0 else (zero, last)
        for k in range(NX):
            at, mid, end = (2 * k + 0) * third, (2 * k + 1) * third, (2 * k + 2) * third
            taps = jnp.concatenate([low[at:mid], low[mid:end] + high[at:mid], high[mid:end]], axis=0).astype(BF16)
            x = lax.rem(at_ref[1] + k, NX)
            size = grad_ref.shape[1]
            for y in range(4):
                rows = taps[y * size : min((y + 1) * size, 3 * third)]
                grad_ref[y * NX + x, 0 : rows.shape[0], :] = rows
                if rows.shape[0] < size:
                    grad_ref[y * NX + x, rows.shape[0] :, :] = jnp.zeros((size - rows.shape[0], group), BF16)
        for d in range(2):
            at = third * ((1 - d) if sign > 0 else d)
            for k in range(NX):
                tall[2 * third * k : 2 * third * (k + 1), :] = held[k, at : at + 2 * third, :]
            part = dot(tall[...], col[...], ((0,), (0,)))
            parts[:, d] = part.astype(BF16).reshape(NZ, width, PLANE)
        for k in range(NZ):
            out_refs[k][...] = parts[lax.rem(at_ref[3] + k, NZ)]

    @pl.when(at_ref[0] == 0)
    def _():
        run(1)

    @pl.when(at_ref[0] == 1)
    def _():
        run(-1)


def finish_kernel(at_ref, *refs):
    own_refs, other_ref, (one_ref, two_ref, near, far) = refs[:4], refs[4], refs[5:]
    taps, channels = one_ref.shape
    _, _, size, group = other_ref.shape
    width = group // NZ
    old = lax.broadcasted_iota(jnp.int32, (channels, channels), 0)
    new = lax.broadcasted_iota(jnp.int32, (channels, channels), 1)
    place = (new // width) % NX * group + new // (NX * width) * width + new % width
    order = (old == place).astype(F32).astype(BF16)

    def put(piece, full, out_ref):
        for k in range(4):
            rows = pl.ds(pl.multiple_of(lax.rem(at_ref[2] + k, 4) * size, 16), size)
            for x in range(NX):
                full[rows, x * group : (x + 1) * group] = piece(k, x)
        out_ref[...] = dot(full[0:taps, :], order, ((1,), (0,)))

    def run(own_out, other_out):
        put(lambda k, x: own_refs[k][x], near, own_out)
        put(lambda k, x: other_ref[k, x], far, other_out)

    @pl.when(at_ref[0] == 0)
    def _():
        run(two_ref, one_ref)

    @pl.when(at_ref[0] == 1)
    def _():
        run(one_ref, two_ref)


def call(kernel, outs, scratch, name, cost, *args):
    vmem = pl.BlockSpec(memory_space=pltpu.VMEM)
    return pl.pallas_call(
        kernel,
        out_shape=tuple(jax.ShapeDtypeStruct(s, t) for s, t in outs),
        in_specs=[pl.BlockSpec(memory_space=pltpu.SMEM)] + [vmem] * (len(args) - 1),
        out_specs=tuple([vmem] * len(outs)),
        scratch_shapes=[pltpu.VMEM(s, t) for s, t in scratch],
        compiler_params=PARAMS,
        cost_estimate=pl.CostEstimate(flops=cost, bytes_accessed=0, transcendentals=0),
        name=name,
    )(*args)


def swap(values):
    return lax.ppermute(values, "spatial", [(0, 1), (1, 0)])


def around(values, axis, step):
    size = lax.axis_size(axis)
    return lax.ppermute(values, axis, [((i + step) % size, i) for i in range(size)])


def body(features, conv_one, conv_two, cotangent):
    width, channels = conv_one.shape[1], conv_one.shape[2]
    at = jnp.stack([lax.axis_index(a) for a in ("spatial", "x", "samples", "z")]).astype(jnp.int32)
    one = conv_one.reshape(27 * width, channels)
    two = conv_two.reshape(27 * width, channels)
    taps = 27 * width
    group = NZ * width
    plane = (2, width, PLANE)
    everyone = (2 * NZ, width, PLANE)
    piece = (7 * width, group)
    work = 4 * 18 * width * channels * PLANE

    pair = jnp.stack([features.reshape(width, PLANE), cotangent.reshape(width, PLANE)])
    pair = jnp.broadcast_to(pair, (NZ,) + plane).reshape(everyone)
    mine = lax.all_to_all(pair, ("z", "spatial"), 0, 0, tiled=True).reshape((NZ,) + plane)

    groups = call(regroup_kernel, [((taps, group), BF16)] * NX, [], "regroup", 2 * taps * channels * channels, at, one, two)
    kernels = [groups[0]] + [around(groups[NX - k], "x", k) for k in range(1, NX)]

    own, *sends, held = call(
        first_kernel,
        [(plane, F32)] + [(plane, BF16)] * (NX - 1) + [((NX, taps, group), BF16)],
        [((NX * 9 * width, 2 * group), BF16), ((2 * group, PLANE), BF16), ((NX * 9 * width, PLANE), F32)],
        "conv_in", work, at, mine, *kernels,
    )
    sends = [around(part, "x", NX - k) for k, part in enumerate(sends, 1)]
    own = own + sum(part.astype(F32) for part in sends)
    held, across = swap(held), swap(mine)

    (send,) = call(act_kernel, [(plane, BF16)], [], "act", 0, at, own, swap(own))
    acts = [send] + [around(send, "x", k) for k in range(1, NX)]
    *parts, grads = call(
        second_kernel,
        [(plane, BF16)] * NZ + [((4 * NX,) + piece, BF16)],
        [((NX * 18 * width, PLANE), BF16), ((NX * 18 * width, group), BF16), ((2 * group, PLANE), BF16), ((NZ,) + plane, BF16)],
        "conv_out", 2 * work, at, *acts, held, across,
    )
    grads = lax.all_to_all(grads, ("samples", "x"), 0, 0, tiled=True)
    parts = [parts[0]] + [around(parts[k], "z", NZ - k) for k in (4, 3, 5, 2, 6, 1, 7)]
    result = sum(part.astype(F32) for part in parts).astype(BF16)
    first = lax.axis_index("spatial") == 0
    ours = jnp.where(first, result[0], result[1])
    theirs = swap(jnp.where(first, result[1], result[0]))

    summed = jnp.sum(grads.reshape((4, NX) + piece).astype(F32), axis=0).astype(BF16)
    pieces = [summed] + [around(summed, "samples", k) for k in (1, 2, 3)]
    others = swap(jnp.stack(pieces))
    grad_one, grad_two = call(
        finish_kernel, [((taps, channels), F32)] * 2, [((28 * width, channels), BF16)] * 2, "finish", 0, at, *pieces, others
    )
    shape = (width, 1, 1, PLANE)
    mixed_out = jnp.where(first, ours, theirs).reshape(shape)
    input_grad = jnp.where(first, theirs, ours).reshape(shape)
    weights = (27, width, channels)
    return mixed_out, input_grad, grad_one.reshape(weights), grad_two.reshape(weights)


def solution(mesh):
    fine = Mesh(
        mesh.devices.reshape(mesh.shape["samples"], NZ, NX, mesh.shape["spatial"]),
        ("samples", "z", "x", "spatial"),
    )
    acts = P(("z", "x"), "samples", "spatial", None)
    kernels = P(None, ("z", "x"), None)
    return jax.shard_map(
        body,
        mesh=fine,
        in_specs=(acts, kernels, kernels, acts),
        out_specs=(acts, acts, kernels, kernels),
        check_vma=False,
    )
```

```python
import jax
import jax.numpy as jnp
from jax import lax
from jax.experimental import pallas as pl
from jax.experimental.pallas import tpu as pltpu
from jax.sharding import Mesh, PartitionSpec as P

SIDE = 32
PLANE = SIDE * SIDE
F32 = jnp.float32
BF16 = jnp.bfloat16
PARAMS = pltpu.CompilerParams(vmem_limit_bytes=40 * 1024 * 1024)
NX = 4
NZ = 8


def masks(rows):
    cell = lax.broadcasted_iota(jnp.int32, (rows, PLANE), 1)
    column = cell & (SIDE - 1)
    row_ok = {-1: cell >= SIDE, 1: cell < PLANE - SIDE}
    col_ok = {-1: column > 0, 1: column < SIDE - 1}
    return row_ok, col_ok


def moved(values, step, ok):
    return jnp.where(ok, pltpu.roll(values, (-step) % PLANE, 1), 0.0)


def dot(lhs, rhs, dims):
    return lax.dot_general(lhs, rhs, (dims, ((), ())), preferred_element_type=F32)


def tap_sum(stack_ref, start, width, sign, ok):
    row_ok, col_ok = ok
    total = None
    for c in range(3):
        part = None
        for b in range(3):
            at = start + (3 * b + c) * width
            term = stack_ref[at : at + width, :]
            drow = sign * (b - 1)
            if drow:
                term = moved(term, SIDE * drow, row_ok[drow])
            part = term if part is None else part + term
        dcol = sign * (c - 1)
        if dcol:
            part = moved(part, dcol, col_ok[dcol])
        total = part if total is None else total + part
    return total


def spread(values, sign, col_ref, start, ok):
    row_ok, col_ok = ok
    width = values.shape[0]
    for c in range(3):
        dcol = sign * (c - 1)
        part = moved(values, dcol, col_ok[dcol]) if dcol else values
        for b in range(3):
            drow = sign * (b - 1)
            term = moved(part, SIDE * drow, row_ok[drow]) if drow else part
            at = start + (3 * b + c) * width
            col_ref[at : at + width, :] = term.astype(BF16)


def regroup_kernel(at_ref, one_ref, two_ref, *out_refs):
    channels = one_ref.shape[1]
    width = channels // (NX * NZ)
    group = NZ * width
    old = lax.broadcasted_iota(jnp.int32, (channels, group), 0)
    new = lax.broadcasted_iota(jnp.int32, (channels, group), 1)

    def run(ref):
        for k in range(NX):
            x = lax.rem(at_ref[1] + k, NX)
            home = (new // width) * (NX * width) + x * width + new % width
            order = (old == home).astype(F32).astype(BF16)
            out_refs[k][...] = dot(ref[...], order, ((1,), (0,))).astype(BF16)

    @pl.when(at_ref[0] == 0)
    def _():
        run(one_ref)

    @pl.when(at_ref[0] == 1)
    def _():
        run(two_ref)


def first_kernel(at_ref, mine_ref, *refs):
    kernels, own_ref, out_refs = refs[:NX], refs[NX], refs[NX + 1 : 2 * NX]
    all_ref, lhs, rhs, stack = refs[2 * NX :]
    width = mine_ref.shape[2]
    group = NZ * width
    third = 9 * width
    ok = masks(width)
    for d in range(2):
        rhs[d * group : (d + 1) * group, :] = mine_ref[:, d].reshape(group, PLANE)
    for k in range(NX):
        all_ref[k] = kernels[k][...]

    def run(sign):
        for d in range(2):
            for k in range(NX):
                for e in range(2):
                    a = 1 + sign * (e - d)
                    lhs[k * third : (k + 1) * third, e * group : (e + 1) * group] = kernels[k][a * third : (a + 1) * third, :]
            stack[...] = dot(lhs[...], rhs[...], ((1,), (0,)))
            for k in range(NX):
                total = tap_sum(stack, k * third, width, sign, ok)
                if k:
                    out_refs[k - 1][d] = total.astype(BF16)
                else:
                    own_ref[d] = total

    @pl.when(at_ref[0] == 0)
    def _():
        run(1)

    @pl.when(at_ref[0] == 1)
    def _():
        run(-1)


def act_kernel(at_ref, own_ref, other_ref, send_ref):
    first = at_ref[0] == 0
    for d in range(2):
        own, other = own_ref[d], other_ref[d]
        pre = jnp.where(first, own, other)
        upstream = jnp.where(first, other, own)
        gate = 1.0 / (1.0 + jnp.exp(-pre))
        hidden = pre * gate
        act = upstream * gate * (1.0 + pre * (1.0 - gate))
        send_ref[d] = jnp.where(first, hidden, act).astype(BF16)


def second_kernel(at_ref, *refs):
    acts, held, across, refs = refs[:NX], refs[NX], refs[NX + 1], refs[NX + 2 :]
    zero_ref, hold_ref, half_ref, give_ref, grad_ref, col, tall, both, parts = refs
    width = held.shape[1] // 27
    third = 9 * width
    group = NZ * width
    ok = masks(width)

    def run(sign):
        for k in range(NX):
            for d in range(2):
                at = 2 * third * k + third * (d if sign > 0 else 1 - d)
                spread(acts[k][d].astype(F32), sign, col, at, ok)
        for d in range(2):
            both[d * group : (d + 1) * group, :] = across[:, d].reshape(group, PLANE)
        grad = dot(col[...], both[...], ((1,), (1,)))
        zero, last = grad[:, 0:group], grad[:, group:]
        low, high = (last, zero) if sign > 0 else (zero, last)
        for k in range(NX):
            at, mid, end = (2 * k + 0) * third, (2 * k + 1) * third, (2 * k + 2) * third
            taps = jnp.concatenate([low[at:mid], low[mid:end] + high[at:mid], high[mid:end]], axis=0).astype(BF16)
            x = lax.rem(at_ref[1] + k, NX)
            size = grad_ref.shape[1]
            for y in range(4):
                rows = taps[y * size : min((y + 1) * size, 3 * third)]
                grad_ref[y * NX + x, 0 : rows.shape[0], :] = rows
                if rows.shape[0] < size:
                    grad_ref[y * NX + x, rows.shape[0] :, :] = jnp.zeros((size - rows.shape[0], group), BF16)
        for d in range(2):
            at = third * ((1 - d) if sign > 0 else d)
            for k in range(NX):
                tall[2 * third * k : 2 * third * (k + 1), :] = held[k, at : at + 2 * third, :]
            part = dot(tall[...], col[...], ((0,), (0,)))
            parts[:, d] = part.astype(BF16).reshape(NZ, width, PLANE)
        core = 0 if sign > 0 else 1
        zero_ref[...] = parts[at_ref[3]]
        for j in range(1, NZ // 2):
            hold_ref[j - 1] = parts[lax.rem(at_ref[3] + (j if sign > 0 else NZ - j), NZ)]
            give_ref[2 * j - 2 : 2 * j] = parts[lax.rem(at_ref[3] + (NZ - j if sign > 0 else j), NZ)]
        half_ref[...] = parts[lax.rem(at_ref[3] + NZ // 2, NZ), core]
        give_ref[NZ - 2] = parts[lax.rem(at_ref[3] + NZ // 2, NZ), 1 - core]

    @pl.when(at_ref[0] == 0)
    def _():
        run(1)

    @pl.when(at_ref[0] == 1)
    def _():
        run(-1)


def sum_kernel(at_ref, *refs):
    near_refs, (far_ref, zero_ref, keep_ref, give_ref) = refs[: NZ // 2 - 1], refs[NZ // 2 - 1 :]

    def run(mine, other):
        for array in range(2):
            kept, given = far_ref[array].astype(F32), None
            for ref in near_refs:
                kept = kept + ref[array, mine].astype(F32)
                term = ref[array, other].astype(F32)
                given = term if given is None else given + term
            if array == 0:
                kept = kept + zero_ref[mine].astype(F32)
                given = given + zero_ref[other].astype(F32)
            keep_ref[array] = kept
            give_ref[array] = given.astype(BF16)

    @pl.when(at_ref[0] == 0)
    def _():
        run(0, 1)

    @pl.when(at_ref[0] == 1)
    def _():
        run(1, 0)


def finish_kernel(at_ref, *refs):
    own_refs, other_ref, (one_ref, two_ref, near, far) = refs[:4], refs[4], refs[5:]
    taps, channels = one_ref.shape
    _, _, size, group = other_ref.shape
    width = group // NZ
    old = lax.broadcasted_iota(jnp.int32, (channels, channels), 0)
    new = lax.broadcasted_iota(jnp.int32, (channels, channels), 1)
    place = (new // width) % NX * group + new // (NX * width) * width + new % width
    order = (old == place).astype(F32).astype(BF16)

    def put(piece, full, out_ref):
        for k in range(4):
            rows = pl.ds(pl.multiple_of(lax.rem(at_ref[2] + k, 4) * size, 16), size)
            for x in range(NX):
                full[rows, x * group : (x + 1) * group] = piece(k, x)
        out_ref[...] = dot(full[0:taps, :], order, ((1,), (0,)))

    def run(own_out, other_out):
        put(lambda k, x: own_refs[k][x], near, own_out)
        put(lambda k, x: other_ref[k, x], far, other_out)

    @pl.when(at_ref[0] == 0)
    def _():
        run(two_ref, one_ref)

    @pl.when(at_ref[0] == 1)
    def _():
        run(one_ref, two_ref)


def call(kernel, outs, scratch, name, cost, *args):
    vmem = pl.BlockSpec(memory_space=pltpu.VMEM)
    return pl.pallas_call(
        kernel,
        out_shape=tuple(jax.ShapeDtypeStruct(s, t) for s, t in outs),
        in_specs=[pl.BlockSpec(memory_space=pltpu.SMEM)] + [vmem] * (len(args) - 1),
        out_specs=tuple([vmem] * len(outs)),
        scratch_shapes=[pltpu.VMEM(s, t) for s, t in scratch],
        compiler_params=PARAMS,
        cost_estimate=pl.CostEstimate(flops=cost, bytes_accessed=0, transcendentals=0),
        name=name,
    )(*args)


def swap(values):
    return lax.ppermute(values, "spatial", [(0, 1), (1, 0)])


def around(values, axis, step):
    size = lax.axis_size(axis)
    return lax.ppermute(values, axis, [((i + step) % size, i) for i in range(size)])


def apart(values, step):
    pairs = [(2 * z, 2 * ((z + step) % NZ)) for z in range(NZ)]
    pairs += [(2 * z + 1, 2 * ((z - step) % NZ) + 1) for z in range(NZ)]
    return lax.ppermute(values, ("z", "spatial"), pairs)


def body(features, conv_one, conv_two, cotangent):
    width, channels = conv_one.shape[1], conv_one.shape[2]
    at = jnp.stack([lax.axis_index(a) for a in ("spatial", "x", "samples", "z")]).astype(jnp.int32)
    one = conv_one.reshape(27 * width, channels)
    two = conv_two.reshape(27 * width, channels)
    taps = 27 * width
    group = NZ * width
    plane = (2, width, PLANE)
    everyone = (2 * NZ, width, PLANE)
    piece = (7 * width, group)
    work = 4 * 18 * width * channels * PLANE

    pair = jnp.stack([features.reshape(width, PLANE), cotangent.reshape(width, PLANE)])
    pair = jnp.broadcast_to(pair, (NZ,) + plane).reshape(everyone)
    mine = lax.all_to_all(pair, ("z", "spatial"), 0, 0, tiled=True).reshape((NZ,) + plane)

    groups = call(regroup_kernel, [((taps, group), BF16)] * NX, [], "regroup", 2 * taps * channels * channels, at, one, two)
    kernels = [groups[0]] + [around(groups[NX - k], "x", k) for k in range(1, NX)]

    own, *sends, held = call(
        first_kernel,
        [(plane, F32)] + [(plane, BF16)] * (NX - 1) + [((NX, taps, group), BF16)],
        [((NX * 9 * width, 2 * group), BF16), ((2 * group, PLANE), BF16), ((NX * 9 * width, PLANE), F32)],
        "conv_in", work, at, mine, *kernels,
    )
    sends = [around(part, "x", NX - k) for k, part in enumerate(sends, 1)]
    own = own + sum(part.astype(F32) for part in sends)
    held, across = swap(held), swap(mine)

    (send,) = call(act_kernel, [(plane, BF16)], [], "act", 0, at, own, swap(own))
    acts = [send] + [around(send, "x", k) for k in range(1, NX)]
    far = NZ // 2
    zero, hold, half, give, grads = call(
        second_kernel,
        [(plane, BF16), ((far - 1,) + plane, BF16), (plane[1:], BF16), ((NZ - 1,) + plane[1:], BF16), ((4 * NX,) + piece, BF16)],
        [((NX * 18 * width, PLANE), BF16), ((NX * 18 * width, group), BF16), ((2 * group, PLANE), BF16), ((NZ,) + plane, BF16)],
        "conv_out", 2 * work, at, *acts, held, across,
    )
    grads = lax.all_to_all(grads, ("samples", "x"), 0, 0, tiled=True)
    got = swap(give)
    sends = [jnp.stack([hold[j - 1], got[2 * j - 2 : 2 * j]]) for j in range(1, far)] + [jnp.stack([half, got[NZ - 2]])]
    came = {j: apart(sends[j - 1], j) for j in range(far, 0, -1)}
    summed = jnp.sum(grads.reshape((4, NX) + piece).astype(F32), axis=0).astype(BF16)
    summed, came[far] = lax.optimization_barrier((summed, came[far]))
    pieces = [summed] + [around(summed, "samples", k) for k in (1, 2, 3)]
    pieces, came = lax.optimization_barrier((pieces, came))
    others = swap(jnp.stack(pieces))
    keep, give = call(
        sum_kernel, [(plane, F32), (plane, BF16)], [], "sum", 0,
        at, *[came[j] for j in range(1, far)], came[far], zero,
    )
    got = swap(give)
    first = lax.axis_index("spatial") == 0
    ours = (keep[0] + got[1].astype(F32)).astype(BF16)
    theirs = (keep[1] + got[0].astype(F32)).astype(BF16)

    grad_one, grad_two = call(
        finish_kernel, [((taps, channels), F32)] * 2, [((28 * width, channels), BF16)] * 2, "finish", 0, at, *pieces, others
    )
    shape = (width, 1, 1, PLANE)
    mixed_out = jnp.where(first, ours, theirs).reshape(shape)
    input_grad = jnp.where(first, theirs, ours).reshape(shape)
    weights = (27, width, channels)
    return mixed_out, input_grad, grad_one.reshape(weights), grad_two.reshape(weights)


def solution(mesh):
    fine = Mesh(
        mesh.devices.reshape(mesh.shape["samples"], NZ, NX, mesh.shape["spatial"]),
        ("samples", "z", "x", "spatial"),
    )
    acts = P(("z", "x"), "samples", "spatial", None)
    kernels = P(None, ("z", "x"), None)
    return jax.shard_map(
        body,
        mesh=fine,
        in_specs=(acts, kernels, kernels, acts),
        out_specs=(acts, acts, kernels, kernels),
        check_vma=False,
    )
```

```python
import jax
import jax.numpy as jnp
from jax import lax
from jax.experimental import pallas as pl
from jax.experimental.pallas import tpu as pltpu
from jax.sharding import Mesh, PartitionSpec as P

SIDE = 32
PLANE = SIDE * SIDE
F32 = jnp.float32
BF16 = jnp.bfloat16
PARAMS = pltpu.CompilerParams(vmem_limit_bytes=40 * 1024 * 1024)
NX = 4
NZ = 8


def masks(rows):
    cell = lax.broadcasted_iota(jnp.int32, (rows, PLANE), 1)
    column = cell & (SIDE - 1)
    row_ok = {-1: cell >= SIDE, 1: cell < PLANE - SIDE}
    col_ok = {-1: column > 0, 1: column < SIDE - 1}
    return row_ok, col_ok


def moved(values, step, ok):
    return jnp.where(ok, pltpu.roll(values, (-step) % PLANE, 1), 0.0)


def dot(lhs, rhs, dims):
    return lax.dot_general(lhs, rhs, (dims, ((), ())), preferred_element_type=F32)


def tap_sum(stack_ref, start, width, sign, ok):
    row_ok, col_ok = ok
    total = None
    for c in range(3):
        part = None
        for b in range(3):
            at = start + (3 * b + c) * width
            term = stack_ref[at : at + width, :]
            drow = sign * (b - 1)
            if drow:
                term = moved(term, SIDE * drow, row_ok[drow])
            part = term if part is None else part + term
        dcol = sign * (c - 1)
        if dcol:
            part = moved(part, dcol, col_ok[dcol])
        total = part if total is None else total + part
    return total


def spread(values, sign, col_ref, start, ok):
    row_ok, col_ok = ok
    width = values.shape[0]
    for c in range(3):
        dcol = sign * (c - 1)
        part = moved(values, dcol, col_ok[dcol]) if dcol else values
        for b in range(3):
            drow = sign * (b - 1)
            term = moved(part, SIDE * drow, row_ok[drow]) if drow else part
            at = start + (3 * b + c) * width
            col_ref[at : at + width, :] = term.astype(BF16)


def regroup_kernel(at_ref, one_ref, two_ref, *out_refs):
    channels = one_ref.shape[1]
    width = channels // (NX * NZ)
    group = NZ * width
    old = lax.broadcasted_iota(jnp.int32, (channels, group), 0)
    new = lax.broadcasted_iota(jnp.int32, (channels, group), 1)

    def run(ref):
        for k in range(NX):
            x = lax.rem(at_ref[1] + k, NX)
            home = (new // width) * (NX * width) + x * width + new % width
            order = (old == home).astype(F32).astype(BF16)
            out_refs[k][...] = dot(ref[...], order, ((1,), (0,))).astype(BF16)

    @pl.when(at_ref[0] == 0)
    def _():
        run(one_ref)

    @pl.when(at_ref[0] == 1)
    def _():
        run(two_ref)


def first_kernel(at_ref, mine_ref, *refs):
    kernels, own_ref, out_refs = refs[:NX], refs[NX], refs[NX + 1 : 2 * NX]
    all_ref, lhs, rhs, stack = refs[2 * NX :]
    width = mine_ref.shape[2]
    group = NZ * width
    third = 9 * width
    ok = masks(width)
    for d in range(2):
        rhs[d * group : (d + 1) * group, :] = mine_ref[:, d].reshape(group, PLANE)
    for k in range(NX):
        all_ref[k] = kernels[k][...]

    def run(sign):
        for d in range(2):
            for k in range(NX):
                for e in range(2):
                    a = 1 + sign * (e - d)
                    lhs[k * third : (k + 1) * third, e * group : (e + 1) * group] = kernels[k][a * third : (a + 1) * third, :]
            stack[...] = dot(lhs[...], rhs[...], ((1,), (0,)))
            for k in range(NX):
                total = tap_sum(stack, k * third, width, sign, ok)
                if k:
                    out_refs[k - 1][d] = total.astype(BF16)
                else:
                    own_ref[d] = total

    @pl.when(at_ref[0] == 0)
    def _():
        run(1)

    @pl.when(at_ref[0] == 1)
    def _():
        run(-1)


def act_kernel(at_ref, own_ref, other_ref, send_ref):
    first = at_ref[0] == 0
    for d in range(2):
        own, other = own_ref[d], other_ref[d]
        pre = jnp.where(first, own, other)
        upstream = jnp.where(first, other, own)
        gate = 1.0 / (1.0 + jnp.exp(-pre))
        hidden = pre * gate
        act = upstream * gate * (1.0 + pre * (1.0 - gate))
        send_ref[d] = jnp.where(first, hidden, act).astype(BF16)


def second_kernel(at_ref, *refs):
    acts, held, across, refs = refs[:NX], refs[NX], refs[NX + 1], refs[NX + 2 :]
    zero_ref, hold_ref, half_ref, give_ref, grad_ref, col, tall, both, parts = refs
    width = held.shape[1] // 27
    third = 9 * width
    group = NZ * width
    ok = masks(width)

    def run(sign):
        for k in range(NX):
            for d in range(2):
                at = 2 * third * k + third * (d if sign > 0 else 1 - d)
                spread(acts[k][d].astype(F32), sign, col, at, ok)
        for d in range(2):
            both[d * group : (d + 1) * group, :] = across[:, d].reshape(group, PLANE)
        grad = dot(col[...], both[...], ((1,), (1,)))
        zero, last = grad[:, 0:group], grad[:, group:]
        low, high = (last, zero) if sign > 0 else (zero, last)
        for k in range(NX):
            at, mid, end = (2 * k + 0) * third, (2 * k + 1) * third, (2 * k + 2) * third
            taps = jnp.concatenate([low[at:mid], low[mid:end] + high[at:mid], high[mid:end]], axis=0).astype(BF16)
            x = lax.rem(at_ref[1] + k, NX)
            size = grad_ref.shape[1]
            for y in range(4):
                rows = taps[y * size : min((y + 1) * size, 3 * third)]
                grad_ref[y * NX + x, 0 : rows.shape[0], :] = rows
                if rows.shape[0] < size:
                    grad_ref[y * NX + x, rows.shape[0] :, :] = jnp.zeros((size - rows.shape[0], group), BF16)
        for d in range(2):
            at = third * ((1 - d) if sign > 0 else d)
            for k in range(NX):
                tall[2 * third * k : 2 * third * (k + 1), :] = held[k, at : at + 2 * third, :]
            part = dot(tall[...], col[...], ((0,), (0,)))
            parts[:, d] = part.astype(BF16).reshape(NZ, width, PLANE)
        core = 0 if sign > 0 else 1
        zero_ref[...] = parts[at_ref[3]]
        for j in range(1, NZ // 2):
            hold_ref[j - 1] = parts[lax.rem(at_ref[3] + (j if sign > 0 else NZ - j), NZ)]
            give_ref[2 * j - 2 : 2 * j] = parts[lax.rem(at_ref[3] + (NZ - j if sign > 0 else j), NZ)]
        half_ref[...] = parts[lax.rem(at_ref[3] + NZ // 2, NZ), core]
        give_ref[NZ - 2] = parts[lax.rem(at_ref[3] + NZ // 2, NZ), 1 - core]

    @pl.when(at_ref[0] == 0)
    def _():
        run(1)

    @pl.when(at_ref[0] == 1)
    def _():
        run(-1)


def sum_kernel(at_ref, *refs):
    near_refs, (far_ref, zero_ref, keep_ref, give_ref) = refs[: NZ // 2 - 1], refs[NZ // 2 - 1 :]

    def run(mine, other):
        for array in range(2):
            kept, given = far_ref[array].astype(F32), None
            for ref in near_refs:
                kept = kept + ref[array, mine].astype(F32)
                term = ref[array, other].astype(F32)
                given = term if given is None else given + term
            if array == 0:
                kept = kept + zero_ref[mine].astype(F32)
                given = given + zero_ref[other].astype(F32)
            keep_ref[array] = kept
            give_ref[array] = given.astype(BF16)

    @pl.when(at_ref[0] == 0)
    def _():
        run(0, 1)

    @pl.when(at_ref[0] == 1)
    def _():
        run(1, 0)


def finish_kernel(at_ref, *refs):
    own_refs, other_ref, keep_ref, got_ref = refs[:4], refs[4], refs[5], refs[6]
    mixed_ref, input_ref, one_ref, two_ref, near, far, wide, cells, sems = refs[7:]
    taps, channels = one_ref.shape
    _, _, size, group = other_ref.shape
    width = group // NZ
    third = taps // 3
    old = lax.broadcasted_iota(jnp.int32, (channels, channels), 0)
    new = lax.broadcasted_iota(jnp.int32, (channels, channels), 1)
    place = (new // width) % NX * group + new // (NX * width) * width + new % width
    order = (old == place).astype(F32).astype(BF16)

    def run(cell_outs, grad_outs):
        copies = []

        def send(source, target):
            copy = pltpu.make_async_copy(source, target, sems.at[len(copies)])
            copy.start()
            copies.append(copy)

        for array in range(2):
            cells[array] = (keep_ref[array] + got_ref[1 - array].astype(F32)).astype(BF16)
            send(cells.at[array], cell_outs[array])
        pieces = (lambda k, x: own_refs[k][x]), (lambda k, x: other_ref[k, x])
        for n, full in enumerate((near, far)):
            for k in range(4):
                rows = pl.ds(pl.multiple_of(lax.rem(at_ref[2] + k, 4) * size, 16), size)
                for x in range(NX):
                    full[rows, x * group : (x + 1) * group] = pieces[n](k, x)
            for a in range(3):
                rows = pl.ds(a * third, third)
                wide[n, rows, :] = dot(full[a * third : (a + 1) * third, :], order, ((1,), (0,)))
                send(wide.at[n, rows], grad_outs[n].at[rows])
        for copy in copies:
            copy.wait()

    @pl.when(at_ref[0] == 0)
    def _():
        run((mixed_ref, input_ref), (two_ref, one_ref))

    @pl.when(at_ref[0] == 1)
    def _():
        run((input_ref, mixed_ref), (one_ref, two_ref))


def call(kernel, outs, scratch, name, cost, *args, out_space=pltpu.VMEM):
    vmem = pl.BlockSpec(memory_space=pltpu.VMEM)
    return pl.pallas_call(
        kernel,
        out_shape=tuple(jax.ShapeDtypeStruct(s, t) for s, t in outs),
        in_specs=[pl.BlockSpec(memory_space=pltpu.SMEM)] + [vmem] * (len(args) - 1),
        out_specs=tuple([pl.BlockSpec(memory_space=out_space)] * len(outs)),
        scratch_shapes=[pltpu.VMEM(*s) if isinstance(s, tuple) else s for s in scratch],
        compiler_params=PARAMS,
        cost_estimate=pl.CostEstimate(flops=cost, bytes_accessed=0, transcendentals=0),
        name=name,
    )(*args)


def swap(values):
    return lax.ppermute(values, "spatial", [(0, 1), (1, 0)])


def around(values, axis, step):
    size = lax.axis_size(axis)
    return lax.ppermute(values, axis, [((i + step) % size, i) for i in range(size)])


def apart(values, step):
    pairs = [(2 * z, 2 * ((z + step) % NZ)) for z in range(NZ)]
    pairs += [(2 * z + 1, 2 * ((z - step) % NZ) + 1) for z in range(NZ)]
    return lax.ppermute(values, ("z", "spatial"), pairs)


def body(features, conv_one, conv_two, cotangent):
    width, channels = conv_one.shape[1], conv_one.shape[2]
    at = jnp.stack([lax.axis_index(a) for a in ("spatial", "x", "samples", "z")]).astype(jnp.int32)
    one = conv_one.reshape(27 * width, channels)
    two = conv_two.reshape(27 * width, channels)
    taps = 27 * width
    group = NZ * width
    plane = (2, width, PLANE)
    everyone = (2 * NZ, width, PLANE)
    piece = (7 * width, group)
    work = 4 * 18 * width * channels * PLANE

    pair = jnp.stack([features.reshape(width, PLANE), cotangent.reshape(width, PLANE)])
    pair = jnp.broadcast_to(pair, (NZ,) + plane).reshape(everyone)
    mine = lax.all_to_all(pair, ("z", "spatial"), 0, 0, tiled=True).reshape((NZ,) + plane)

    groups = call(regroup_kernel, [((taps, group), BF16)] * NX, [], "regroup", 2 * taps * channels * channels, at, one, two)
    kernels = [groups[0]] + [around(groups[NX - k], "x", k) for k in range(1, NX)]

    own, *sends, held = call(
        first_kernel,
        [(plane, F32)] + [(plane, BF16)] * (NX - 1) + [((NX, taps, group), BF16)],
        [((NX * 9 * width, 2 * group), BF16), ((2 * group, PLANE), BF16), ((NX * 9 * width, PLANE), F32)],
        "conv_in", work, at, mine, *kernels,
    )
    sends = [around(part, "x", NX - k) for k, part in enumerate(sends, 1)]
    own = own + sum(part.astype(F32) for part in sends)
    held, across = swap(held), swap(mine)

    (send,) = call(act_kernel, [(plane, BF16)], [], "act", 0, at, own, swap(own))
    acts = [send] + [around(send, "x", k) for k in range(1, NX)]
    far = NZ // 2
    zero, hold, half, give, grads = call(
        second_kernel,
        [(plane, BF16), ((far - 1,) + plane, BF16), (plane[1:], BF16), ((NZ - 1,) + plane[1:], BF16), ((4 * NX,) + piece, BF16)],
        [((NX * 18 * width, PLANE), BF16), ((NX * 18 * width, group), BF16), ((2 * group, PLANE), BF16), ((NZ,) + plane, BF16)],
        "conv_out", 2 * work, at, *acts, held, across,
    )
    grads = lax.all_to_all(grads, ("samples", "x"), 0, 0, tiled=True)
    got = swap(give)
    sends = [jnp.stack([hold[j - 1], got[2 * j - 2 : 2 * j]]) for j in range(1, far)] + [jnp.stack([half, got[NZ - 2]])]
    came = {j: apart(sends[j - 1], j) for j in range(far, 0, -1)}
    summed = jnp.sum(grads.reshape((4, NX) + piece).astype(F32), axis=0).astype(BF16)
    summed, came[far] = lax.optimization_barrier((summed, came[far]))
    pieces = [summed] + [around(summed, "samples", k) for k in (1, 2, 3)]
    pieces, came = lax.optimization_barrier((pieces, came))
    others = swap(jnp.stack(pieces))
    keep, give = call(
        sum_kernel, [(plane, F32), (plane, BF16)], [], "sum", 0, at, *[came[j] for j in range(1, far)], came[far], zero
    )
    mixed_out, input_grad, grad_one, grad_two = call(
        finish_kernel,
        [((width, PLANE), BF16)] * 2 + [((taps, channels), F32)] * 2,
        [((28 * width, channels), BF16)] * 2
        + [((2, taps, channels), F32), (plane, BF16), pltpu.SemaphoreType.DMA((8,))],
        "finish", 0, at, *pieces, others, keep, swap(give), out_space=pl.ANY,
    )
    shape = (width, 1, 1, PLANE)
    weights = (27, width, channels)
    return mixed_out.reshape(shape), input_grad.reshape(shape), grad_one.reshape(weights), grad_two.reshape(weights)


def solution(mesh):
    fine = Mesh(
        mesh.devices.reshape(mesh.shape["samples"], NZ, NX, mesh.shape["spatial"]),
        ("samples", "z", "x", "spatial"),
    )
    acts = P(("z", "x"), "samples", "spatial", None)
    kernels = P(None, ("z", "x"), None)
    return jax.shard_map(
        body,
        mesh=fine,
        in_specs=(acts, kernels, kernels, acts),
        out_specs=(acts, acts, kernels, kernels),
        check_vma=False,
    )
```

```python
import jax
import jax.numpy as jnp
from jax import lax
from jax.experimental import pallas as pl
from jax.experimental.pallas import tpu as pltpu
from jax.sharding import Mesh, PartitionSpec as P

SIDE = 32
PLANE = SIDE * SIDE
F32 = jnp.float32
BF16 = jnp.bfloat16
PARAMS = pltpu.CompilerParams(vmem_limit_bytes=40 * 1024 * 1024)
NX = 4
NZ = 8


def masks(rows):
    cell = lax.broadcasted_iota(jnp.int32, (rows, PLANE), 1)
    column = cell & (SIDE - 1)
    row_ok = {-1: cell >= SIDE, 1: cell < PLANE - SIDE}
    col_ok = {-1: column > 0, 1: column < SIDE - 1}
    return row_ok, col_ok


def moved(values, step, ok):
    return jnp.where(ok, pltpu.roll(values, (-step) % PLANE, 1), 0.0)


def dot(lhs, rhs, dims):
    return lax.dot_general(lhs, rhs, (dims, ((), ())), preferred_element_type=F32)


def tap_sum(stack_ref, start, width, sign, ok):
    row_ok, col_ok = ok
    total = None
    for c in range(3):
        part = None
        for b in range(3):
            at = start + (3 * b + c) * width
            term = stack_ref[at : at + width, :]
            drow = sign * (b - 1)
            if drow:
                term = moved(term, SIDE * drow, row_ok[drow])
            part = term if part is None else part + term
        dcol = sign * (c - 1)
        if dcol:
            part = moved(part, dcol, col_ok[dcol])
        total = part if total is None else total + part
    return total


def spread(values, sign, col_ref, start, ok):
    row_ok, col_ok = ok
    width = values.shape[0]
    for c in range(3):
        dcol = sign * (c - 1)
        part = moved(values, dcol, col_ok[dcol]) if dcol else values
        for b in range(3):
            drow = sign * (b - 1)
            term = moved(part, SIDE * drow, row_ok[drow]) if drow else part
            at = start + (3 * b + c) * width
            col_ref[at : at + width, :] = term.astype(BF16)


def regroup_kernel(at_ref, one_ref, two_ref, *out_refs):
    channels = one_ref.shape[1]
    width = channels // (NX * NZ)
    group = NZ * width
    low = width.bit_length() - 1
    old = lax.broadcasted_iota(jnp.int32, (channels, group), 0)
    new = lax.broadcasted_iota(jnp.int32, (channels, group), 1)
    for part in range(NX):
        column = new + part * group
        place = (column >> low & 3) * group + (column >> low + 2 << low) + (column & (width - 1))
        out_refs[NX][:, part * group : (part + 1) * group] = (old == place).astype(F32).astype(BF16)

    def run(ref):
        for k in range(NX):
            x = lax.rem(at_ref[1] + k, NX)
            home = (new >> low << low + 2) + (x << low) + (new & (width - 1))
            order = (old == home).astype(F32).astype(BF16)
            out_refs[k][...] = dot(ref[...], order, ((1,), (0,))).astype(BF16)

    @pl.when(at_ref[0] == 0)
    def _():
        run(one_ref)

    @pl.when(at_ref[0] == 1)
    def _():
        run(two_ref)


def first_kernel(at_ref, mine_ref, *refs):
    kernels, own_ref, out_refs = refs[:NX], refs[NX], refs[NX + 1 : 2 * NX]
    all_ref, lhs, rhs, stack = refs[2 * NX :]
    width = mine_ref.shape[2]
    group = NZ * width
    third = 9 * width
    ok = masks(width)
    for d in range(2):
        rhs[d * group : (d + 1) * group, :] = mine_ref[:, d].reshape(group, PLANE)
    for k in range(NX):
        all_ref[k] = kernels[k][...]

    def run(sign):
        for d in range(2):
            for k in range(NX):
                for e in range(2):
                    a = 1 + sign * (e - d)
                    lhs[k * third : (k + 1) * third, e * group : (e + 1) * group] = kernels[k][a * third : (a + 1) * third, :]
            stack[...] = dot(lhs[...], rhs[...], ((1,), (0,)))
            for k in range(NX):
                total = tap_sum(stack, k * third, width, sign, ok)
                if k:
                    out_refs[k - 1][d] = total.astype(BF16)
                else:
                    own_ref[d] = total

    @pl.when(at_ref[0] == 0)
    def _():
        run(1)

    @pl.when(at_ref[0] == 1)
    def _():
        run(-1)


def act_kernel(at_ref, own_ref, other_ref, send_ref):
    first = at_ref[0] == 0
    for d in range(2):
        own, other = own_ref[d], other_ref[d]
        pre = jnp.where(first, own, other)
        upstream = jnp.where(first, other, own)
        gate = 1.0 / (1.0 + jnp.exp(-pre))
        hidden = pre * gate
        act = upstream * gate * (1.0 + pre * (1.0 - gate))
        send_ref[d] = jnp.where(first, hidden, act).astype(BF16)


def second_kernel(at_ref, *refs):
    acts, held, across, refs = (refs[0], refs[1], refs[3], refs[2]), refs[NX], refs[NX + 1], refs[NX + 2 :]
    zero_ref, hold_ref, half_ref, give_ref, grad_ref, col, tall, both, parts = refs
    width = held.shape[1] // 27
    third = 9 * width
    group = NZ * width
    ok = masks(width)

    def run(sign):
        for k in range(NX):
            for d in range(2):
                at = 2 * third * k + third * (d if sign > 0 else 1 - d)
                spread(acts[k][d].astype(F32), sign, col, at, ok)
        for d in range(2):
            both[d * group : (d + 1) * group, :] = across[:, d].reshape(group, PLANE)
        grad = dot(col[...], both[...], ((1,), (1,)))
        zero, last = grad[:, 0:group], grad[:, group:]
        low, high = (last, zero) if sign > 0 else (zero, last)
        for k in range(NX):
            at, mid, end = (2 * k + 0) * third, (2 * k + 1) * third, (2 * k + 2) * third
            taps = jnp.concatenate([low[at:mid], low[mid:end] + high[at:mid], high[mid:end]], axis=0).astype(BF16)
            x = lax.rem(at_ref[1] + k, NX)
            size = grad_ref.shape[1]
            for y in range(4):
                rows = taps[y * size : min((y + 1) * size, 3 * third)]
                grad_ref[y * NX + x, 0 : rows.shape[0], :] = rows
                if rows.shape[0] < size:
                    grad_ref[y * NX + x, rows.shape[0] :, :] = jnp.zeros((size - rows.shape[0], group), BF16)
        for d in range(2):
            at = third * ((1 - d) if sign > 0 else d)
            for k in range(NX):
                tall[2 * third * k : 2 * third * (k + 1), :] = held[k, at : at + 2 * third, :]
            part = dot(tall[...], col[...], ((0,), (0,)))
            parts[:, d] = part.astype(BF16).reshape(NZ, width, PLANE)
        core = 0 if sign > 0 else 1
        zero_ref[...] = parts[at_ref[3]]
        for j in range(1, NZ // 2):
            hold_ref[j - 1] = parts[lax.rem(at_ref[3] + (j if sign > 0 else NZ - j), NZ)]
            give_ref[2 * j - 2 : 2 * j] = parts[lax.rem(at_ref[3] + (NZ - j if sign > 0 else j), NZ)]
        half_ref[...] = parts[lax.rem(at_ref[3] + NZ // 2, NZ), core]
        give_ref[NZ - 2] = parts[lax.rem(at_ref[3] + NZ // 2, NZ), 1 - core]

    @pl.when(at_ref[0] == 0)
    def _():
        run(1)

    @pl.when(at_ref[0] == 1)
    def _():
        run(-1)


def sum_kernel(at_ref, *refs):
    near_refs, (far_ref, zero_ref, keep_ref, give_ref) = refs[: NZ // 2 - 1], refs[NZ // 2 - 1 :]

    def run(mine, other):
        for array in range(2):
            kept, given = far_ref[array].astype(F32), None
            for ref in near_refs:
                kept = kept + ref[array, mine].astype(F32)
                term = ref[array, other].astype(F32)
                given = term if given is None else given + term
            if array == 0:
                kept = kept + zero_ref[mine].astype(F32)
                given = given + zero_ref[other].astype(F32)
            keep_ref[array] = kept
            give_ref[array] = given.astype(BF16)

    @pl.when(at_ref[0] == 0)
    def _():
        run(0, 1)

    @pl.when(at_ref[0] == 1)
    def _():
        run(1, 0)


def finish_kernel(at_ref, *refs):
    own_refs, other_ref, keep_ref, got_ref, order_ref = refs[:4], *refs[4:8]
    mixed_ref, input_ref, one_ref, two_ref, near, far, wide, cells, sems = refs[8:]
    taps, channels = one_ref.shape
    _, _, size, group = other_ref.shape
    third = taps // 3

    def run(cell_outs, grad_outs):
        copies = []

        def send(source, target):
            copy = pltpu.make_async_copy(source, target, sems.at[len(copies)])
            copy.start()
            copies.append(copy)

        for array in range(2):
            cells[array] = (keep_ref[array] + got_ref[1 - array].astype(F32)).astype(BF16)
            send(cells.at[array], cell_outs[array])
        pieces = (lambda k, x: own_refs[k][x]), (lambda k, x: other_ref[k, x])
        for n, full in enumerate((near, far)):
            for k in range(4):
                rows = pl.ds(pl.multiple_of(lax.rem(at_ref[2] + (0, 1, 3, 2)[k], 4) * size, 16), size)
                for x in range(NX):
                    full[rows, x * group : (x + 1) * group] = pieces[n](k, x)
            for a in range(3):
                rows = pl.ds(a * third, third)
                wide[n, rows, :] = dot(full[a * third : (a + 1) * third, :], order_ref[...], ((1,), (0,)))
                send(wide.at[n, rows], grad_outs[n].at[rows])
        for copy in copies:
            copy.wait()

    @pl.when(at_ref[0] == 0)
    def _():
        run((mixed_ref, input_ref), (two_ref, one_ref))

    @pl.when(at_ref[0] == 1)
    def _():
        run((input_ref, mixed_ref), (one_ref, two_ref))


def call(kernel, outs, scratch, name, cost, *args, out_space=pltpu.VMEM):
    vmem = pl.BlockSpec(memory_space=pltpu.VMEM)
    return pl.pallas_call(
        kernel,
        out_shape=tuple(jax.ShapeDtypeStruct(s, t) for s, t in outs),
        in_specs=[pl.BlockSpec(memory_space=pltpu.SMEM)] + [vmem] * (len(args) - 1),
        out_specs=tuple([pl.BlockSpec(memory_space=out_space)] * len(outs)),
        scratch_shapes=[pltpu.VMEM(*s) if isinstance(s, tuple) else s for s in scratch],
        compiler_params=PARAMS,
        cost_estimate=pl.CostEstimate(flops=cost, bytes_accessed=0, transcendentals=0),
        name=name,
    )(*args)


def swap(values):
    return lax.ppermute(values, "spatial", [(0, 1), (1, 0)])


def around(values, axis, step):
    size = lax.axis_size(axis)
    return lax.ppermute(values, axis, [((i + step) % size, i) for i in range(size)])


def apart(values, step):
    pairs = [(2 * z, 2 * ((z + step) % NZ)) for z in range(NZ)]
    pairs += [(2 * z + 1, 2 * ((z - step) % NZ) + 1) for z in range(NZ)]
    return lax.ppermute(values, ("z", "spatial"), pairs)


def body(features, conv_one, conv_two, cotangent):
    width, channels = conv_one.shape[1], conv_one.shape[2]
    at = jnp.stack([lax.axis_index(a) for a in ("spatial", "x", "samples", "z")]).astype(jnp.int32)
    one = conv_one.reshape(27 * width, channels)
    two = conv_two.reshape(27 * width, channels)
    taps = 27 * width
    group = NZ * width
    plane = (2, width, PLANE)
    everyone = (2 * NZ, width, PLANE)
    piece = (7 * width, group)
    work = 4 * 18 * width * channels * PLANE

    pair = jnp.stack([features.reshape(width, PLANE), cotangent.reshape(width, PLANE)])
    pair = jnp.broadcast_to(pair, (NZ,) + plane).reshape(everyone)
    mine = lax.all_to_all(pair, ("z", "spatial"), 0, 0, tiled=True).reshape((NZ,) + plane)

    *groups, order = call(regroup_kernel, [((taps, group), BF16)] * NX + [((channels, channels), BF16)], [], "regroup", 2 * taps * channels * channels, at, one, two)
    kernels = [groups[0]] + [around(groups[NX - k], "x", k) for k in range(1, NX)]

    own, *sends, held = call(
        first_kernel,
        [(plane, F32)] + [(plane, BF16)] * (NX - 1) + [((NX, taps, group), BF16)],
        [((NX * 9 * width, 2 * group), BF16), ((2 * group, PLANE), BF16), ((NX * 9 * width, PLANE), F32)],
        "conv_in", work, at, mine, *kernels,
    )
    sends = [around(sends[k - 1], "x", NX - k) for k in (2, 1, 3)]
    own = own + sum(part.astype(F32) for part in sends)
    held, across = swap(held), swap(mine)

    (send,) = call(act_kernel, [(plane, BF16)], [], "act", 0, at, own, swap(own))
    acts = {k: around(send, "x", k) for k in (1, 3, 2)}
    far = NZ // 2
    zero, hold, half, give, grads = call(
        second_kernel,
        [(plane, BF16), ((far - 1,) + plane, BF16), (plane[1:], BF16), ((NZ - 1,) + plane[1:], BF16), ((4 * NX,) + piece, BF16)],
        [((NX * 18 * width, PLANE), BF16), ((NX * 18 * width, group), BF16), ((2 * group, PLANE), BF16), ((NZ,) + plane, BF16)],
        "conv_out", 2 * work, at, send, acts[1], acts[3], acts[2], held, across,
    )
    grads = lax.all_to_all(grads, ("samples", "x"), 0, 0, tiled=True)
    got = swap(give)
    sends = [jnp.stack([hold[j - 1], got[2 * j - 2 : 2 * j]]) for j in range(1, far)] + [jnp.stack([half, got[NZ - 2]])]
    came = {j: apart(sends[j - 1], j) for j in range(far, 0, -1)}
    summed = jnp.sum(grads.reshape((4, NX) + piece).astype(F32), axis=0).astype(BF16)
    summed, came[far] = lax.optimization_barrier((summed, came[far]))
    pieces = {k: around(summed, "samples", k) for k in (1, 3, 2)}
    pieces = [summed] + [pieces[k] for k in (1, 3, 2)]
    pieces, came = lax.optimization_barrier((pieces, came))
    others = swap(jnp.stack(pieces))
    keep, give = call(
        sum_kernel, [(plane, F32), (plane, BF16)], [], "sum", 0, at, *[came[j] for j in range(1, far)], came[far], zero
    )
    mixed_out, input_grad, grad_one, grad_two = call(
        finish_kernel,
        [((width, PLANE), BF16)] * 2 + [((taps, channels), F32)] * 2,
        [((28 * width, channels), BF16)] * 2
        + [((2, taps, channels), F32), (plane, BF16), pltpu.SemaphoreType.DMA((8,))],
        "finish", 0, at, *pieces, others, keep, swap(give), order, out_space=pl.ANY,
    )
    shape = (width, 1, 1, PLANE)
    weights = (27, width, channels)
    return mixed_out.reshape(shape), input_grad.reshape(shape), grad_one.reshape(weights), grad_two.reshape(weights)


def solution(mesh):
    fine = Mesh(
        mesh.devices.reshape(mesh.shape["samples"], NZ, NX, mesh.shape["spatial"]),
        ("samples", "z", "x", "spatial"),
    )
    acts = P(("z", "x"), "samples", "spatial", None)
    kernels = P(None, ("z", "x"), None)
    return jax.shard_map(
        body,
        mesh=fine,
        in_specs=(acts, kernels, kernels, acts),
        out_specs=(acts, acts, kernels, kernels),
        check_vma=False,
    )
```

```python
import jax
import jax.numpy as jnp
from jax import lax
from jax.experimental import pallas as pl
from jax.experimental.pallas import tpu as pltpu
from jax.sharding import Mesh, PartitionSpec as P

SIDE = 32
PLANE = SIDE * SIDE
F32 = jnp.float32
BF16 = jnp.bfloat16
PARAMS = pltpu.CompilerParams(vmem_limit_bytes=40 * 1024 * 1024)
NX = 4
NZ = 8


def masks(rows):
    cell = lax.broadcasted_iota(jnp.int32, (rows, PLANE), 1)
    column = cell & (SIDE - 1)
    row_ok = {-1: cell >= SIDE, 1: cell < PLANE - SIDE}
    col_ok = {-1: column > 0, 1: column < SIDE - 1}
    return row_ok, col_ok


def moved(values, step, ok):
    return jnp.where(ok, pltpu.roll(values, (-step) % PLANE, 1), 0.0)


def dot(lhs, rhs, dims):
    return lax.dot_general(lhs, rhs, (dims, ((), ())), preferred_element_type=F32)


def tap_sum(stack_ref, start, width, sign, ok):
    row_ok, col_ok = ok
    total = None
    for c in range(3):
        part = None
        for b in range(3):
            at = start + (3 * b + c) * width
            term = stack_ref[at : at + width, :]
            drow = sign * (b - 1)
            if drow:
                term = moved(term, SIDE * drow, row_ok[drow])
            part = term if part is None else part + term
        dcol = sign * (c - 1)
        if dcol:
            part = moved(part, dcol, col_ok[dcol])
        total = part if total is None else total + part
    return total


def spread(values, sign, col_ref, start, ok):
    row_ok, col_ok = ok
    width = values.shape[0]
    for c in range(3):
        dcol = sign * (c - 1)
        part = moved(values, dcol, col_ok[dcol]) if dcol else values
        for b in range(3):
            drow = sign * (b - 1)
            term = moved(part, SIDE * drow, row_ok[drow]) if drow else part
            at = start + (3 * b + c) * width
            col_ref[at : at + width, :] = term.astype(BF16)


def regroup_kernel(at_ref, one_ref, two_ref, *out_refs):
    channels = one_ref.shape[1]
    width = channels // (NX * NZ)
    group = NZ * width
    low = width.bit_length() - 1
    old = lax.broadcasted_iota(jnp.int32, (channels, group), 0)
    new = lax.broadcasted_iota(jnp.int32, (channels, group), 1)
    for part in range(NX):
        column = new + part * group
        place = (column >> low & 3) * group + (column >> low + 2 << low) + (column & (width - 1))
        out_refs[NX][:, part * group : (part + 1) * group] = (old == place).astype(F32).astype(BF16)

    def run(ref):
        for k in range(NX):
            x = lax.rem(at_ref[1] + k, NX)
            home = (new >> low << low + 2) + (x << low) + (new & (width - 1))
            order = (old == home).astype(F32).astype(BF16)
            out_refs[k][...] = dot(ref[...], order, ((1,), (0,))).astype(BF16)

    @pl.when(at_ref[0] == 0)
    def _():
        run(one_ref)

    @pl.when(at_ref[0] == 1)
    def _():
        run(two_ref)


def first_kernel(at_ref, pair_ref, other_ref, *refs):
    near_refs, far_ref, got_ref, refs = refs[: NZ // 2 - 1], refs[NZ // 2 - 1], refs[NZ // 2], refs[NZ // 2 + 1 :]
    kernels, own_ref, out_refs = refs[:NX], refs[NX], refs[NX + 1 : 2 * NX]
    all_ref, mine_ref, lhs, rhs, stack = refs[2 * NX :]
    width = pair_ref.shape[1]
    group = NZ * width
    third = 9 * width
    ok = masks(width)

    def put(step, plane, values):
        z = lax.rem(at_ref[3] + (step + NZ), NZ)
        rhs[pl.ds(pl.multiple_of(plane * group + z * width, 16), width), :] = values
        mine_ref[z, plane] = values

    def place(core, ahead):
        put(0, core, pair_ref[core])
        put(0, 1 - core, other_ref[core])
        for j in range(1, NZ // 2):
            put(ahead * j, core, near_refs[j - 1][0, core])
            put(ahead * j, 1 - core, near_refs[j - 1][1, core])
            put(-ahead * j, 1 - core, got_ref[2 * j - 2])
            put(-ahead * j, core, got_ref[2 * j - 1])
        put(NZ // 2, core, far_ref[core])
        put(NZ // 2, 1 - core, got_ref[NZ - 2])

    for k in range(NX):
        all_ref[k] = kernels[k][...]

    def run(sign):
        for d in range(2):
            for k in range(NX):
                for e in range(2):
                    a = 1 + sign * (e - d)
                    lhs[k * third : (k + 1) * third, e * group : (e + 1) * group] = kernels[k][a * third : (a + 1) * third, :]
            stack[...] = dot(lhs[...], rhs[...], ((1,), (0,)))
            for k in range(NX):
                total = tap_sum(stack, k * third, width, sign, ok)
                if k:
                    out_refs[k - 1][d] = total.astype(BF16)
                else:
                    own_ref[d] = total

    @pl.when(at_ref[0] == 0)
    def _():
        place(0, -1)
        run(1)

    @pl.when(at_ref[0] == 1)
    def _():
        place(1, 1)
        run(-1)


def act_kernel(at_ref, own_ref, other_ref, send_ref):
    first = at_ref[0] == 0
    for d in range(2):
        own, other = own_ref[d], other_ref[d]
        pre = jnp.where(first, own, other)
        upstream = jnp.where(first, other, own)
        gate = 1.0 / (1.0 + jnp.exp(-pre))
        hidden = pre * gate
        act = upstream * gate * (1.0 + pre * (1.0 - gate))
        send_ref[d] = jnp.where(first, hidden, act).astype(BF16)


def second_kernel(at_ref, *refs):
    acts, held, across, refs = (refs[0], refs[1], refs[3], refs[2]), refs[NX], refs[NX + 1], refs[NX + 2 :]
    zero_ref, hold_ref, half_ref, give_ref, grad_ref, col, tall, both, parts = refs
    width = held.shape[1] // 27
    third = 9 * width
    group = NZ * width
    ok = masks(width)

    def run(sign):
        for k in range(NX):
            for d in range(2):
                at = 2 * third * k + third * (d if sign > 0 else 1 - d)
                spread(acts[k][d].astype(F32), sign, col, at, ok)
        for d in range(2):
            both[d * group : (d + 1) * group, :] = across[:, d].reshape(group, PLANE)
        grad = dot(col[...], both[...], ((1,), (1,)))
        zero, last = grad[:, 0:group], grad[:, group:]
        low, high = (last, zero) if sign > 0 else (zero, last)
        for k in range(NX):
            at, mid, end = (2 * k + 0) * third, (2 * k + 1) * third, (2 * k + 2) * third
            taps = jnp.concatenate([low[at:mid], low[mid:end] + high[at:mid], high[mid:end]], axis=0).astype(BF16)
            x = lax.rem(at_ref[1] + k, NX)
            size = grad_ref.shape[1]
            for y in range(4):
                rows = taps[y * size : min((y + 1) * size, 3 * third)]
                grad_ref[y * NX + x, 0 : rows.shape[0], :] = rows
                if rows.shape[0] < size:
                    grad_ref[y * NX + x, rows.shape[0] :, :] = jnp.zeros((size - rows.shape[0], group), BF16)
        for d in range(2):
            at = third * ((1 - d) if sign > 0 else d)
            for k in range(NX):
                tall[2 * third * k : 2 * third * (k + 1), :] = held[k, at : at + 2 * third, :]
            part = dot(tall[...], col[...], ((0,), (0,)))
            parts[:, d] = part.astype(BF16).reshape(NZ, width, PLANE)
        core = 0 if sign > 0 else 1
        zero_ref[...] = parts[at_ref[3]]
        for j in range(1, NZ // 2):
            hold_ref[j - 1] = parts[lax.rem(at_ref[3] + (j if sign > 0 else NZ - j), NZ)]
            give_ref[2 * j - 2 : 2 * j] = parts[lax.rem(at_ref[3] + (NZ - j if sign > 0 else j), NZ)]
        half_ref[...] = parts[lax.rem(at_ref[3] + NZ // 2, NZ), core]
        give_ref[NZ - 2] = parts[lax.rem(at_ref[3] + NZ // 2, NZ), 1 - core]

    @pl.when(at_ref[0] == 0)
    def _():
        run(1)

    @pl.when(at_ref[0] == 1)
    def _():
        run(-1)


def sum_kernel(at_ref, *refs):
    near_refs, (far_ref, zero_ref, keep_ref, give_ref) = refs[: NZ // 2 - 1], refs[NZ // 2 - 1 :]

    def run(mine, other):
        for array in range(2):
            kept, given = far_ref[array].astype(F32), None
            for ref in near_refs:
                kept = kept + ref[array, mine].astype(F32)
                term = ref[array, other].astype(F32)
                given = term if given is None else given + term
            if array == 0:
                kept = kept + zero_ref[mine].astype(F32)
                given = given + zero_ref[other].astype(F32)
            keep_ref[array] = kept
            give_ref[array] = given.astype(BF16)

    @pl.when(at_ref[0] == 0)
    def _():
        run(0, 1)

    @pl.when(at_ref[0] == 1)
    def _():
        run(1, 0)


def finish_kernel(at_ref, *refs):
    own_refs, other_ref, keep_ref, got_ref, order_ref = refs[:4], *refs[4:8]
    mixed_ref, input_ref, one_ref, two_ref, near, far, wide, cells, sems = refs[8:]
    taps, channels = one_ref.shape
    _, _, size, group = other_ref.shape
    third = taps // 3

    def run(cell_outs, grad_outs):
        copies = []

        def send(source, target):
            copy = pltpu.make_async_copy(source, target, sems.at[len(copies)])
            copy.start()
            copies.append(copy)

        for array in range(2):
            cells[array] = (keep_ref[array] + got_ref[1 - array].astype(F32)).astype(BF16)
            send(cells.at[array], cell_outs[array])
        pieces = (lambda k, x: own_refs[k][x]), (lambda k, x: other_ref[k, x])
        for n, full in enumerate((near, far)):
            for k in range(4):
                rows = pl.ds(pl.multiple_of(lax.rem(at_ref[2] + (0, 1, 3, 2)[k], 4) * size, 16), size)
                for x in range(NX):
                    full[rows, x * group : (x + 1) * group] = pieces[n](k, x)
            for a in range(3):
                rows = pl.ds(a * third, third)
                wide[n, rows, :] = dot(full[a * third : (a + 1) * third, :], order_ref[...], ((1,), (0,)))
                send(wide.at[n, rows], grad_outs[n].at[rows])
        for copy in copies:
            copy.wait()

    @pl.when(at_ref[0] == 0)
    def _():
        run((mixed_ref, input_ref), (two_ref, one_ref))

    @pl.when(at_ref[0] == 1)
    def _():
        run((input_ref, mixed_ref), (one_ref, two_ref))


def call(kernel, outs, scratch, name, cost, *args, out_space=pltpu.VMEM):
    vmem = pl.BlockSpec(memory_space=pltpu.VMEM)
    return pl.pallas_call(
        kernel,
        out_shape=tuple(jax.ShapeDtypeStruct(s, t) for s, t in outs),
        in_specs=[pl.BlockSpec(memory_space=pltpu.SMEM)] + [vmem] * (len(args) - 1),
        out_specs=tuple([pl.BlockSpec(memory_space=out_space)] * len(outs)),
        scratch_shapes=[pltpu.VMEM(*s) if isinstance(s, tuple) else s for s in scratch],
        compiler_params=PARAMS,
        cost_estimate=pl.CostEstimate(flops=cost, bytes_accessed=0, transcendentals=0),
        name=name,
    )(*args)


def swap(values):
    return lax.ppermute(values, "spatial", [(0, 1), (1, 0)])


def around(values, axis, step):
    size = lax.axis_size(axis)
    return lax.ppermute(values, axis, [((i + step) % size, i) for i in range(size)])


def apart(values, step):
    pairs = [(2 * z, 2 * ((z + step) % NZ)) for z in range(NZ)]
    pairs += [(2 * z + 1, 2 * ((z - step) % NZ) + 1) for z in range(NZ)]
    return lax.ppermute(values, ("z", "spatial"), pairs)


def body(features, conv_one, conv_two, cotangent):
    width, channels = conv_one.shape[1], conv_one.shape[2]
    at = jnp.stack([lax.axis_index(a) for a in ("spatial", "x", "samples", "z")]).astype(jnp.int32)
    one = conv_one.reshape(27 * width, channels)
    two = conv_two.reshape(27 * width, channels)
    taps = 27 * width
    group = NZ * width
    plane = (2, width, PLANE)
    piece = (7 * width, group)
    work = 4 * 18 * width * channels * PLANE

    far = NZ // 2
    first = lax.axis_index("spatial") == 0
    pair = jnp.stack([features.reshape(width, PLANE), cotangent.reshape(width, PLANE)])
    came = {far: apart(pair, far)}
    other = swap(pair)
    both = jnp.stack([pair, other])
    came.update({j: apart(both, j) for j in range(far - 1, 0, -1)})
    *groups, order = call(regroup_kernel, [((taps, group), BF16)] * NX + [((channels, channels), BF16)], [], "regroup", 2 * taps * channels * channels, at, one, two)
    kernels = [groups[0]] + [around(groups[NX - k], "x", k) for k in range(1, NX)]
    came, kernels = lax.optimization_barrier((came, kernels))

    give = [jnp.where(first, came[j][:, 1], came[j][:, 0]) for j in range(1, far)]
    give.append(jnp.where(first, came[far][1], came[far][0])[None])
    got = swap(jnp.concatenate(give))

    own, *sends, held, mine = call(
        first_kernel,
        [(plane, F32)] + [(plane, BF16)] * (NX - 1) + [((NX, taps, group), BF16), ((NZ,) + plane, BF16)],
        [((NX * 9 * width, 2 * group), BF16), ((2 * group, PLANE), BF16), ((NX * 9 * width, PLANE), F32)],
        "conv_in", work, at, pair, other, *[came[j] for j in range(1, far)], came[far], got, *kernels,
    )
    sends = [around(sends[k - 1], "x", NX - k) for k in (2, 1, 3)]
    own = own + sum(part.astype(F32) for part in sends)
    held, across = swap(held), swap(mine)

    (send,) = call(act_kernel, [(plane, BF16)], [], "act", 0, at, own, swap(own))
    acts = {k: around(send, "x", k) for k in (1, 3, 2)}
    zero, hold, half, give, grads = call(
        second_kernel,
        [(plane, BF16), ((far - 1,) + plane, BF16), (plane[1:], BF16), ((NZ - 1,) + plane[1:], BF16), ((4 * NX,) + piece, BF16)],
        [((NX * 18 * width, PLANE), BF16), ((NX * 18 * width, group), BF16), ((2 * group, PLANE), BF16), ((NZ,) + plane, BF16)],
        "conv_out", 2 * work, at, send, acts[1], acts[3], acts[2], held, across,
    )
    grads = lax.all_to_all(grads, ("samples", "x"), 0, 0, tiled=True)
    got = swap(give)
    sends = [jnp.stack([hold[j - 1], got[2 * j - 2 : 2 * j]]) for j in range(1, far)] + [jnp.stack([half, got[NZ - 2]])]
    came = {j: apart(sends[j - 1], j) for j in range(far, 0, -1)}
    summed = jnp.sum(grads.reshape((4, NX) + piece).astype(F32), axis=0).astype(BF16)
    summed, came[far] = lax.optimization_barrier((summed, came[far]))
    pieces = {k: around(summed, "samples", k) for k in (1, 3, 2)}
    pieces = [summed] + [pieces[k] for k in (1, 3, 2)]
    pieces, came = lax.optimization_barrier((pieces, came))
    others = swap(jnp.stack(pieces))
    keep, give = call(
        sum_kernel, [(plane, F32), (plane, BF16)], [], "sum", 0, at, *[came[j] for j in range(1, far)], came[far], zero
    )
    mixed_out, input_grad, grad_one, grad_two = call(
        finish_kernel,
        [((width, PLANE), BF16)] * 2 + [((taps, channels), F32)] * 2,
        [((28 * width, channels), BF16)] * 2
        + [((2, taps, channels), F32), (plane, BF16), pltpu.SemaphoreType.DMA((8,))],
        "finish", 0, at, *pieces, others, keep, swap(give), order, out_space=pl.ANY,
    )
    shape = (width, 1, 1, PLANE)
    weights = (27, width, channels)
    return mixed_out.reshape(shape), input_grad.reshape(shape), grad_one.reshape(weights), grad_two.reshape(weights)


def solution(mesh):
    fine = Mesh(
        mesh.devices.reshape(mesh.shape["samples"], NZ, NX, mesh.shape["spatial"]),
        ("samples", "z", "x", "spatial"),
    )
    acts = P(("z", "x"), "samples", "spatial", None)
    kernels = P(None, ("z", "x"), None)
    return jax.shard_map(
        body,
        mesh=fine,
        in_specs=(acts, kernels, kernels, acts),
        out_specs=(acts, acts, kernels, kernels),
        check_vma=False,
    )
```

```python
import jax
import jax.numpy as jnp
from jax import lax
from jax.experimental import pallas as pl
from jax.experimental.pallas import tpu as pltpu
from jax.sharding import Mesh, PartitionSpec as P

SIDE = 32
PLANE = SIDE * SIDE
F32 = jnp.float32
BF16 = jnp.bfloat16
PARAMS = pltpu.CompilerParams(vmem_limit_bytes=40 * 1024 * 1024)
NX = 4
NZ = 8


def masks(rows):
    cell = lax.broadcasted_iota(jnp.int32, (rows, PLANE), 1)
    column = cell & (SIDE - 1)
    row_ok = {-1: cell >= SIDE, 1: cell < PLANE - SIDE}
    col_ok = {-1: column > 0, 1: column < SIDE - 1}
    return row_ok, col_ok


def moved(values, step, ok):
    return jnp.where(ok, pltpu.roll(values, (-step) % PLANE, 1), 0.0)


def dot(lhs, rhs, dims):
    return lax.dot_general(lhs, rhs, (dims, ((), ())), preferred_element_type=F32)


def tap_sum(stack_ref, start, width, sign, ok):
    row_ok, col_ok = ok
    total = None
    for c in range(3):
        part = None
        for b in range(3):
            at = start + (3 * b + c) * width
            term = stack_ref[at : at + width, :]
            drow = sign * (b - 1)
            if drow:
                term = moved(term, SIDE * drow, row_ok[drow])
            part = term if part is None else part + term
        dcol = sign * (c - 1)
        if dcol:
            part = moved(part, dcol, col_ok[dcol])
        total = part if total is None else total + part
    return total


def spread(values, sign, col_ref, start, ok):
    row_ok, col_ok = ok
    width = values.shape[0]
    for c in range(3):
        dcol = sign * (c - 1)
        part = moved(values, dcol, col_ok[dcol]) if dcol else values
        for b in range(3):
            drow = sign * (b - 1)
            term = moved(part, SIDE * drow, row_ok[drow]) if drow else part
            at = start + (3 * b + c) * width
            col_ref[at : at + width, :] = term.astype(BF16)


def regroup_kernel(at_ref, one_ref, two_ref, *out_refs):
    channels = one_ref.shape[1]
    width = channels // (NX * NZ)
    group = NZ * width
    low = width.bit_length() - 1
    old = lax.broadcasted_iota(jnp.int32, (channels, group), 0)
    new = lax.broadcasted_iota(jnp.int32, (channels, group), 1)
    for part in range(NX):
        column = new + part * group
        place = (column >> low & 3) * group + (column >> low + 2 << low) + (column & (width - 1))
        out_refs[NX][:, part * group : (part + 1) * group] = (old == place).astype(F32).astype(BF16)

    def run(ref):
        for k in range(NX):
            x = lax.rem(at_ref[1] + k, NX)
            home = (new >> low << low + 2) + (x << low) + (new & (width - 1))
            order = (old == home).astype(F32).astype(BF16)
            out_refs[k][...] = dot(ref[...], order, ((1,), (0,))).astype(BF16)

    @pl.when(at_ref[0] == 0)
    def _():
        run(one_ref)

    @pl.when(at_ref[0] == 1)
    def _():
        run(two_ref)


def first_kernel(at_ref, pair_ref, other_ref, *refs):
    near_refs, far_ref, got_ref, refs = refs[: NZ // 2 - 1], refs[NZ // 2 - 1], refs[NZ // 2], refs[NZ // 2 + 1 :]
    kernels, own_ref, out_refs = refs[:NX], refs[NX], refs[NX + 1 : 2 * NX]
    all_ref, mine_ref, lhs, rhs, stack = refs[2 * NX :]
    width = pair_ref.shape[1]
    group = NZ * width
    third = 9 * width
    ok = masks(width)

    def put(step, plane, values):
        z = lax.rem(at_ref[3] + (step + NZ), NZ)
        rhs[pl.ds(pl.multiple_of(plane * group + z * width, 16), width), :] = values
        mine_ref[z, plane] = values

    def place(core, ahead):
        put(0, core, pair_ref[core])
        put(0, 1 - core, other_ref[core])
        for j in range(1, NZ // 2):
            put(ahead * j, core, near_refs[j - 1][0, core])
            put(ahead * j, 1 - core, near_refs[j - 1][1, core])
            put(-ahead * j, 1 - core, got_ref[2 * j - 2])
            put(-ahead * j, core, got_ref[2 * j - 1])
        put(NZ // 2, core, far_ref[core])
        put(NZ // 2, 1 - core, got_ref[NZ - 2])

    for k in range(NX):
        all_ref[k] = kernels[k][...]

    def run(sign):
        for d in range(2):
            for k in range(NX):
                for e in range(2):
                    a = 1 + sign * (e - d)
                    lhs[k * third : (k + 1) * third, e * group : (e + 1) * group] = kernels[k][a * third : (a + 1) * third, :]
            stack[...] = dot(lhs[...], rhs[...], ((1,), (0,)))
            for k in range(NX):
                total = tap_sum(stack, k * third, width, sign, ok)
                if k:
                    out_refs[k - 1][d] = total.astype(BF16)
                else:
                    own_ref[d] = total

    @pl.when(at_ref[0] == 0)
    def _():
        place(0, -1)
        run(1)

    @pl.when(at_ref[0] == 1)
    def _():
        place(1, 1)
        run(-1)


def act_kernel(at_ref, own_ref, other_ref, send_ref):
    first = at_ref[0] == 0
    for d in range(2):
        own, other = own_ref[d], other_ref[d]
        pre = jnp.where(first, own, other)
        upstream = jnp.where(first, other, own)
        gate = 1.0 / (1.0 + jnp.exp(-pre))
        hidden = pre * gate
        act = upstream * gate * (1.0 + pre * (1.0 - gate))
        send_ref[d] = jnp.where(first, hidden, act).astype(BF16)


def second_kernel(at_ref, *refs):
    acts, held, across, refs = (refs[0], refs[1], refs[3], refs[2]), refs[NX], refs[NX + 1], refs[NX + 2 :]
    zero_ref, hold_ref, half_ref, give_ref, grad_ref, col, tall, both, parts = refs
    width = held.shape[1] // 27
    third = 9 * width
    group = NZ * width
    ok = masks(width)

    def run(sign):
        for k in range(NX):
            for d in range(2):
                at = 2 * third * k + third * (d if sign > 0 else 1 - d)
                spread(acts[k][d].astype(F32), sign, col, at, ok)
        for d in range(2):
            both[d * group : (d + 1) * group, :] = across[:, d].reshape(group, PLANE)
        grad = dot(col[...], both[...], ((1,), (1,)))
        zero, last = grad[:, 0:group], grad[:, group:]
        low, high = (last, zero) if sign > 0 else (zero, last)
        for k in range(NX):
            at, mid, end = (2 * k + 0) * third, (2 * k + 1) * third, (2 * k + 2) * third
            taps = jnp.concatenate([low[at:mid], low[mid:end] + high[at:mid], high[mid:end]], axis=0).astype(BF16)
            x = lax.rem(at_ref[1] + k, NX)
            size = grad_ref.shape[1]
            for y in range(4):
                rows = taps[y * size : min((y + 1) * size, 3 * third)]
                grad_ref[y * NX + x, 0 : rows.shape[0], :] = rows
                if rows.shape[0] < size:
                    grad_ref[y * NX + x, rows.shape[0] :, :] = jnp.zeros((size - rows.shape[0], group), BF16)
        for d in range(2):
            at = third * ((1 - d) if sign > 0 else d)
            for k in range(NX):
                tall[2 * third * k : 2 * third * (k + 1), :] = held[k, at : at + 2 * third, :]
            part = dot(tall[...], col[...], ((0,), (0,)))
            parts[:, d] = part.astype(BF16).reshape(NZ, width, PLANE)
        core = 0 if sign > 0 else 1
        zero_ref[...] = parts[at_ref[3]]
        for j in range(1, NZ // 2):
            hold_ref[j - 1] = parts[lax.rem(at_ref[3] + (j if sign > 0 else NZ - j), NZ)]
            give_ref[2 * j - 2 : 2 * j] = parts[lax.rem(at_ref[3] + (NZ - j if sign > 0 else j), NZ)]
        half_ref[...] = parts[lax.rem(at_ref[3] + NZ // 2, NZ), core]
        give_ref[NZ - 2] = parts[lax.rem(at_ref[3] + NZ // 2, NZ), 1 - core]

    @pl.when(at_ref[0] == 0)
    def _():
        run(1)

    @pl.when(at_ref[0] == 1)
    def _():
        run(-1)


def sum_kernel(at_ref, *refs):
    near_refs, (far_ref, zero_ref, keep_ref, give_ref) = refs[: NZ // 2 - 1], refs[NZ // 2 - 1 :]

    def run(mine, other):
        for array in range(2):
            kept, given = far_ref[array].astype(F32), None
            for ref in near_refs:
                kept = kept + ref[array, mine].astype(F32)
                term = ref[array, other].astype(F32)
                given = term if given is None else given + term
            if array == 0:
                kept = kept + zero_ref[mine].astype(F32)
                given = given + zero_ref[other].astype(F32)
            keep_ref[array] = kept
            give_ref[array] = given.astype(BF16)

    @pl.when(at_ref[0] == 0)
    def _():
        run(0, 1)

    @pl.when(at_ref[0] == 1)
    def _():
        run(1, 0)


def finish_kernel(at_ref, *refs):
    own_refs, other_ref, keep_ref, got_ref, order_ref = refs[:4], *refs[4:8]
    mixed_ref, input_ref, one_ref, two_ref, near, far, wide, cells, sems = refs[8:]
    taps, channels = one_ref.shape
    _, _, size, group = other_ref.shape
    third = taps // 3

    def run(cell_outs, grad_outs):
        copies = []

        def send(source, target):
            copy = pltpu.make_async_copy(source, target, sems.at[len(copies)])
            copy.start()
            copies.append(copy)

        for array in range(2):
            cells[array] = (keep_ref[array] + got_ref[1 - array].astype(F32)).astype(BF16)
            send(cells.at[array], cell_outs[array])
        pieces = (lambda k, x: own_refs[k][x]), (lambda k, x: other_ref[k, x])
        for n, full in enumerate((near, far)):
            for k in range(4):
                rows = pl.ds(pl.multiple_of(lax.rem(at_ref[2] + (0, 1, 3, 2)[k], 4) * size, 16), size)
                for x in range(NX):
                    full[rows, x * group : (x + 1) * group] = pieces[n](k, x)
            for a in range(3):
                rows = pl.ds(a * third, third)
                wide[n, rows, :] = dot(full[a * third : (a + 1) * third, :], order_ref[...], ((1,), (0,)))
                send(wide.at[n, rows], grad_outs[n].at[rows])
        for copy in copies:
            copy.wait()

    @pl.when(at_ref[0] == 0)
    def _():
        run((mixed_ref, input_ref), (two_ref, one_ref))

    @pl.when(at_ref[0] == 1)
    def _():
        run((input_ref, mixed_ref), (one_ref, two_ref))


def call(kernel, outs, scratch, name, cost, *args, out_space=pltpu.VMEM):
    vmem = pl.BlockSpec(memory_space=pltpu.VMEM)
    return pl.pallas_call(
        kernel,
        out_shape=tuple(jax.ShapeDtypeStruct(s, t) for s, t in outs),
        in_specs=[pl.BlockSpec(memory_space=pltpu.SMEM)] + [vmem] * (len(args) - 1),
        out_specs=tuple([pl.BlockSpec(memory_space=out_space)] * len(outs)),
        scratch_shapes=[pltpu.VMEM(*s) if isinstance(s, tuple) else s for s in scratch],
        compiler_params=PARAMS,
        cost_estimate=pl.CostEstimate(flops=cost, bytes_accessed=0, transcendentals=0),
        name=name,
    )(*args)


def swap(values):
    return lax.ppermute(values, "spatial", [(0, 1), (1, 0)])


def around(values, axis, step):
    size = lax.axis_size(axis)
    return lax.ppermute(values, axis, [((i + step) % size, i) for i in range(size)])


def apart(values, step):
    pairs = [(2 * z, 2 * ((z + step) % NZ)) for z in range(NZ)]
    pairs += [(2 * z + 1, 2 * ((z - step) % NZ) + 1) for z in range(NZ)]
    return lax.ppermute(values, ("z", "spatial"), pairs)


def body(features, conv_one, conv_two, cotangent):
    width, channels = conv_one.shape[1], conv_one.shape[2]
    at = jnp.stack([lax.axis_index(a) for a in ("spatial", "x", "samples", "z")]).astype(jnp.int32)
    one = conv_one.reshape(27 * width, channels)
    two = conv_two.reshape(27 * width, channels)
    taps = 27 * width
    group = NZ * width
    plane = (2, width, PLANE)
    piece = (7 * width, group)
    work = 4 * 18 * width * channels * PLANE

    far = NZ // 2
    first = lax.axis_index("spatial") == 0
    pair = jnp.stack([features.reshape(width, PLANE), cotangent.reshape(width, PLANE)])
    came = {far: apart(pair, far)}
    other = swap(pair)
    both = jnp.stack([pair, other])
    came.update({j: apart(both, j) for j in range(far - 1, 0, -1)})
    one, two, came[1] = lax.optimization_barrier((one, two, came[1]))
    *groups, order = call(regroup_kernel, [((taps, group), BF16)] * NX + [((channels, channels), BF16)], [], "regroup", 2 * taps * channels * channels, at, one, two)
    kernels = [groups[0]] + [around(groups[NX - k], "x", k) for k in range(1, NX)]
    came, kernels = lax.optimization_barrier((came, kernels))

    give = [jnp.where(first, came[j][:, 1], came[j][:, 0]) for j in range(1, far)]
    give.append(jnp.where(first, came[far][1], came[far][0])[None])
    got = swap(jnp.concatenate(give))

    own, *sends, held, mine = call(
        first_kernel,
        [(plane, F32)] + [(plane, BF16)] * (NX - 1) + [((NX, taps, group), BF16), ((NZ,) + plane, BF16)],
        [((NX * 9 * width, 2 * group), BF16), ((2 * group, PLANE), BF16), ((NX * 9 * width, PLANE), F32)],
        "conv_in", work, at, pair, other, *[came[j] for j in range(1, far)], came[far], got, *kernels,
    )
    sends = [around(sends[k - 1], "x", NX - k) for k in (2, 1, 3)]
    own = own + sum(part.astype(F32) for part in sends)
    held, across = swap(held), swap(mine)

    (send,) = call(act_kernel, [(plane, BF16)], [], "act", 0, at, own, swap(own))
    acts = {k: around(send, "x", k) for k in (1, 3, 2)}
    zero, hold, half, give, grads = call(
        second_kernel,
        [(plane, BF16), ((far - 1,) + plane, BF16), (plane[1:], BF16), ((NZ - 1,) + plane[1:], BF16), ((4 * NX,) + piece, BF16)],
        [((NX * 18 * width, PLANE), BF16), ((NX * 18 * width, group), BF16), ((2 * group, PLANE), BF16), ((NZ,) + plane, BF16)],
        "conv_out", 2 * work, at, send, acts[1], acts[3], acts[2], held, across,
    )
    grads = lax.all_to_all(grads, ("samples", "x"), 0, 0, tiled=True)
    got = swap(give)
    sends = [jnp.stack([hold[j - 1], got[2 * j - 2 : 2 * j]]) for j in range(1, far)] + [jnp.stack([half, got[NZ - 2]])]
    came = {j: apart(sends[j - 1], j) for j in range(far, 0, -1)}
    summed = jnp.sum(grads.reshape((4, NX) + piece).astype(F32), axis=0).astype(BF16)
    summed, came[far] = lax.optimization_barrier((summed, came[far]))
    pieces = {k: around(summed, "samples", k) for k in (1, 3, 2)}
    pieces = [summed] + [pieces[k] for k in (1, 3, 2)]
    pieces, came = lax.optimization_barrier((pieces, came))
    others = swap(jnp.stack(pieces))
    keep, give = call(
        sum_kernel, [(plane, F32), (plane, BF16)], [], "sum", 0, at, *[came[j] for j in range(1, far)], came[far], zero
    )
    mixed_out, input_grad, grad_one, grad_two = call(
        finish_kernel,
        [((width, PLANE), BF16)] * 2 + [((taps, channels), F32)] * 2,
        [((28 * width, channels), BF16)] * 2
        + [((2, taps, channels), F32), (plane, BF16), pltpu.SemaphoreType.DMA((8,))],
        "finish", 0, at, *pieces, others, keep, swap(give), order, out_space=pl.ANY,
    )
    shape = (width, 1, 1, PLANE)
    weights = (27, width, channels)
    return mixed_out.reshape(shape), input_grad.reshape(shape), grad_one.reshape(weights), grad_two.reshape(weights)


def solution(mesh):
    fine = Mesh(
        mesh.devices.reshape(mesh.shape["samples"], NZ, NX, mesh.shape["spatial"]),
        ("samples", "z", "x", "spatial"),
    )
    acts = P(("z", "x"), "samples", "spatial", None)
    kernels = P(None, ("z", "x"), None)
    return jax.shard_map(
        body,
        mesh=fine,
        in_specs=(acts, kernels, kernels, acts),
        out_specs=(acts, acts, kernels, kernels),
        check_vma=False,
    )
```

```python
import jax
import jax.numpy as jnp
from jax import lax
from jax.experimental import pallas as pl
from jax.experimental.pallas import tpu as pltpu
from jax.sharding import Mesh, PartitionSpec as P

SIDE = 32
PLANE = SIDE * SIDE
F32 = jnp.float32
BF16 = jnp.bfloat16
PARAMS = pltpu.CompilerParams(vmem_limit_bytes=40 * 1024 * 1024)
NX = 4
NZ = 8


def masks(rows):
    cell = lax.broadcasted_iota(jnp.int32, (rows, PLANE), 1)
    column = cell & (SIDE - 1)
    row_ok = {-1: cell >= SIDE, 1: cell < PLANE - SIDE}
    col_ok = {-1: column > 0, 1: column < SIDE - 1}
    return row_ok, col_ok


def moved(values, step, ok):
    return jnp.where(ok, pltpu.roll(values, (-step) % PLANE, 1), 0.0)


def dot(lhs, rhs, dims):
    return lax.dot_general(lhs, rhs, (dims, ((), ())), preferred_element_type=F32)


def tap_sum(stack_ref, start, width, sign, ok):
    row_ok, col_ok = ok
    total = None
    for c in range(3):
        part = None
        for b in range(3):
            at = start + (3 * b + c) * width
            term = stack_ref[at : at + width, :]
            drow = sign * (b - 1)
            if drow:
                term = moved(term, SIDE * drow, row_ok[drow])
            part = term if part is None else part + term
        dcol = sign * (c - 1)
        if dcol:
            part = moved(part, dcol, col_ok[dcol])
        total = part if total is None else total + part
    return total


def spread(values, sign, col_ref, start, ok):
    row_ok, col_ok = ok
    width = values.shape[0]
    for c in range(3):
        dcol = sign * (c - 1)
        part = moved(values, dcol, col_ok[dcol]) if dcol else values
        for b in range(3):
            drow = sign * (b - 1)
            term = moved(part, SIDE * drow, row_ok[drow]) if drow else part
            at = start + (3 * b + c) * width
            col_ref[at : at + width, :] = term.astype(BF16)


def regroup_kernel(at_ref, one_ref, two_ref, *out_refs):
    channels = one_ref.shape[1]
    width = channels // (NX * NZ)
    group = NZ * width
    low = width.bit_length() - 1
    old = lax.broadcasted_iota(jnp.int32, (channels, group), 0)
    new = lax.broadcasted_iota(jnp.int32, (channels, group), 1)
    for part in range(NX):
        column = new + part * group
        place = (column >> low & 3) * group + (column >> low + 2 << low) + (column & (width - 1))
        out_refs[NX][:, part * group : (part + 1) * group] = (old == place).astype(F32).astype(BF16)

    def run(ref):
        for k in range(NX):
            x = lax.rem(at_ref[1] + k, NX)
            home = (new >> low << low + 2) + (x << low) + (new & (width - 1))
            order = (old == home).astype(F32).astype(BF16)
            out_refs[k][...] = dot(ref[...], order, ((1,), (0,))).astype(BF16)

    @pl.when(at_ref[0] == 0)
    def _():
        run(one_ref)

    @pl.when(at_ref[0] == 1)
    def _():
        run(two_ref)


def first_kernel(at_ref, pair_ref, other_ref, *refs):
    near_refs, far_ref, got_ref, refs = refs[: NZ // 2 - 1], refs[NZ // 2 - 1], refs[NZ // 2], refs[NZ // 2 + 1 :]
    kernels, own_ref, out_refs = refs[:NX], refs[NX], refs[NX + 1 : 2 * NX]
    all_ref, mine_ref, lhs, rhs, stack = refs[2 * NX :]
    width = pair_ref.shape[1]
    group = NZ * width
    third = 9 * width
    ok = masks(width)

    def put(step, plane, values):
        z = lax.rem(at_ref[3] + (step + NZ), NZ)
        rhs[pl.ds(pl.multiple_of(plane * group + z * width, 16), width), :] = values
        mine_ref[z, plane] = values

    def place(core, ahead):
        put(0, core, pair_ref[core])
        put(0, 1 - core, other_ref[core])
        for j in range(1, NZ // 2):
            put(ahead * j, core, near_refs[j - 1][0, core])
            put(ahead * j, 1 - core, near_refs[j - 1][1, core])
            put(-ahead * j, 1 - core, got_ref[2 * j - 2])
            put(-ahead * j, core, got_ref[2 * j - 1])
        put(NZ // 2, core, far_ref[core])
        put(NZ // 2, 1 - core, got_ref[NZ - 2])

    for k in range(NX):
        all_ref[k] = kernels[k][...]

    def run(sign):
        for d in range(2):
            for k in range(NX):
                for e in range(2):
                    a = 1 + sign * (e - d)
                    lhs[k * third : (k + 1) * third, e * group : (e + 1) * group] = kernels[k][a * third : (a + 1) * third, :]
            stack[...] = dot(lhs[...], rhs[...], ((1,), (0,)))
            for k in range(NX):
                total = tap_sum(stack, k * third, width, sign, ok)
                if k:
                    out_refs[k - 1][d] = total.astype(BF16)
                else:
                    own_ref[d] = total

    @pl.when(at_ref[0] == 0)
    def _():
        place(0, -1)
        run(1)

    @pl.when(at_ref[0] == 1)
    def _():
        place(1, 1)
        run(-1)


def act_kernel(at_ref, own_ref, other_ref, send_ref):
    first = at_ref[0] == 0
    for d in range(2):
        own, other = own_ref[d], other_ref[d]
        pre = jnp.where(first, own, other)
        upstream = jnp.where(first, other, own)
        gate = 1.0 / (1.0 + jnp.exp(-pre))
        hidden = pre * gate
        act = upstream * gate * (1.0 + pre * (1.0 - gate))
        send_ref[d] = jnp.where(first, hidden, act).astype(BF16)


def second_kernel(at_ref, *refs):
    acts, held, across, refs = (refs[0], refs[1], refs[3], refs[2]), refs[NX], refs[NX + 1], refs[NX + 2 :]
    zero_ref, hold_ref, half_ref, give_ref, grad_ref, col, tall, both, parts = refs
    width = held.shape[1] // 27
    third = 9 * width
    group = NZ * width
    ok = masks(width)

    def run(sign):
        for k in range(NX):
            for d in range(2):
                at = 2 * third * k + third * (d if sign > 0 else 1 - d)
                spread(acts[k][d].astype(F32), sign, col, at, ok)
        for d in range(2):
            both[d * group : (d + 1) * group, :] = across[:, d].reshape(group, PLANE)
        grad = dot(col[...], both[...], ((1,), (1,)))
        zero, last = grad[:, 0:group], grad[:, group:]
        low, high = (last, zero) if sign > 0 else (zero, last)
        for k in range(NX):
            at, mid, end = (2 * k + 0) * third, (2 * k + 1) * third, (2 * k + 2) * third
            taps = jnp.concatenate([low[at:mid], low[mid:end] + high[at:mid], high[mid:end]], axis=0).astype(BF16)
            x = lax.rem(at_ref[1] + k, NX)
            size = grad_ref.shape[1]
            for y in range(4):
                rows = taps[y * size : min((y + 1) * size, 3 * third)]
                grad_ref[y * NX + x, 0 : rows.shape[0], :] = rows
                if rows.shape[0] < size:
                    grad_ref[y * NX + x, rows.shape[0] :, :] = jnp.zeros((size - rows.shape[0], group), BF16)
        for d in range(2):
            at = third * ((1 - d) if sign > 0 else d)
            for k in range(NX):
                tall[2 * third * k : 2 * third * (k + 1), :] = held[k, at : at + 2 * third, :]
            part = dot(tall[...], col[...], ((0,), (0,)))
            parts[:, d] = part.astype(BF16).reshape(NZ, width, PLANE)
        core = 0 if sign > 0 else 1
        zero_ref[...] = parts[at_ref[3]]
        for j in range(1, NZ // 2):
            hold_ref[j - 1] = parts[lax.rem(at_ref[3] + (j if sign > 0 else NZ - j), NZ)]
            give_ref[2 * j - 2 : 2 * j] = parts[lax.rem(at_ref[3] + (NZ - j if sign > 0 else j), NZ)]
        half_ref[...] = parts[lax.rem(at_ref[3] + NZ // 2, NZ), core]
        give_ref[NZ - 2] = parts[lax.rem(at_ref[3] + NZ // 2, NZ), 1 - core]

    @pl.when(at_ref[0] == 0)
    def _():
        run(1)

    @pl.when(at_ref[0] == 1)
    def _():
        run(-1)


def sum_kernel(at_ref, *refs):
    near_refs, (far_ref, zero_ref, keep_ref, give_ref) = refs[: NZ // 2 - 1], refs[NZ // 2 - 1 :]

    def run(mine, other):
        for array in range(2):
            kept, given = far_ref[array].astype(F32), None
            for ref in near_refs:
                kept = kept + ref[array, mine].astype(F32)
                term = ref[array, other].astype(F32)
                given = term if given is None else given + term
            if array == 0:
                kept = kept + zero_ref[mine].astype(F32)
                given = given + zero_ref[other].astype(F32)
            keep_ref[array] = kept
            give_ref[array] = given.astype(BF16)

    @pl.when(at_ref[0] == 0)
    def _():
        run(0, 1)

    @pl.when(at_ref[0] == 1)
    def _():
        run(1, 0)


def put_grad(at_ref, piece, full, wide, order_ref, target, send):
    taps, channels = wide.shape
    size, third, group = full.shape[0] // 4, taps // 3, channels // NX
    for k in range(4):
        rows = pl.ds(pl.multiple_of(lax.rem(at_ref[2] + (0, 1, 3, 2)[k], 4) * size, 16), size)
        for x in range(NX):
            full[rows, x * group : (x + 1) * group] = piece(k, x)
    for a in range(3):
        rows = pl.ds(a * third, third)
        wide[rows, :] = dot(full[a * third : (a + 1) * third, :], order_ref[...], ((1,), (0,)))
        send(wide.at[rows], target.at[rows])


def sender(sems, copies):
    def send(source, target):
        copy = pltpu.make_async_copy(source, target, sems.at[len(copies)])
        copy.start()
        copies.append(copy)

    return send


def own_kernel(at_ref, p0_ref, p1_ref, p2_ref, p3_ref, order_ref, one_ref, two_ref, full, wide, sems):
    own_refs = (p0_ref, p1_ref, p2_ref, p3_ref)

    def run(target):
        copies = []
        put_grad(at_ref, lambda k, x: own_refs[k][x], full, wide, order_ref, target, sender(sems, copies))
        for copy in copies:
            copy.wait()

    @pl.when(at_ref[0] == 0)
    def _():
        run(two_ref)

    @pl.when(at_ref[0] == 1)
    def _():
        run(one_ref)


def finish_kernel(at_ref, other_ref, keep_ref, got_ref, order_ref, _one, _two, mixed_ref, input_ref, one_ref, two_ref, full, wide, cells, sems):
    def run(cell_outs, target):
        copies = []
        send = sender(sems, copies)
        for array in range(2):
            cells[array] = (keep_ref[array] + got_ref[1 - array].astype(F32)).astype(BF16)
            send(cells.at[array], cell_outs[array])
        put_grad(at_ref, lambda k, x: other_ref[k, x], full, wide, order_ref, target, send)
        for copy in copies:
            copy.wait()

    @pl.when(at_ref[0] == 0)
    def _():
        run((mixed_ref, input_ref), one_ref)

    @pl.when(at_ref[0] == 1)
    def _():
        run((input_ref, mixed_ref), two_ref)


def call(kernel, outs, scratch, name, cost, *args, out_space=pltpu.VMEM, within=0):
    vmem = pl.BlockSpec(memory_space=pltpu.VMEM)
    return pl.pallas_call(
        kernel,
        out_shape=tuple(jax.ShapeDtypeStruct(s, t) for s, t in outs),
        in_specs=[pl.BlockSpec(memory_space=pltpu.SMEM)] + [vmem] * (len(args) - 1 - within) + [pl.BlockSpec(memory_space=pl.ANY)] * within,
        input_output_aliases={len(args) - i: len(outs) - i for i in range(1, within + 1)},
        out_specs=tuple([pl.BlockSpec(memory_space=out_space)] * len(outs)),
        scratch_shapes=[pltpu.VMEM(*s) if isinstance(s, tuple) else s for s in scratch],
        compiler_params=PARAMS,
        cost_estimate=pl.CostEstimate(flops=cost, bytes_accessed=0, transcendentals=0),
        name=name,
    )(*args)


def swap(values):
    return lax.ppermute(values, "spatial", [(0, 1), (1, 0)])


def around(values, axis, step):
    size = lax.axis_size(axis)
    return lax.ppermute(values, axis, [((i + step) % size, i) for i in range(size)])


def apart(values, step):
    pairs = [(2 * z, 2 * ((z + step) % NZ)) for z in range(NZ)]
    pairs += [(2 * z + 1, 2 * ((z - step) % NZ) + 1) for z in range(NZ)]
    return lax.ppermute(values, ("z", "spatial"), pairs)


def body(features, conv_one, conv_two, cotangent):
    width, channels = conv_one.shape[1], conv_one.shape[2]
    at = jnp.stack([lax.axis_index(a) for a in ("spatial", "x", "samples", "z")]).astype(jnp.int32)
    one = conv_one.reshape(27 * width, channels)
    two = conv_two.reshape(27 * width, channels)
    taps = 27 * width
    group = NZ * width
    plane = (2, width, PLANE)
    piece = (7 * width, group)
    work = 4 * 18 * width * channels * PLANE

    far = NZ // 2
    first = lax.axis_index("spatial") == 0
    pair = jnp.stack([features.reshape(width, PLANE), cotangent.reshape(width, PLANE)])
    came = {far: apart(pair, far)}
    other = swap(pair)
    both = jnp.stack([pair, other])
    came.update({j: apart(both, j) for j in range(far - 1, 0, -1)})
    one, two, came[1] = lax.optimization_barrier((one, two, came[1]))
    *groups, order = call(regroup_kernel, [((taps, group), BF16)] * NX + [((channels, channels), BF16)], [], "regroup", 2 * taps * channels * channels, at, one, two)
    kernels = [groups[0]] + [around(groups[NX - k], "x", k) for k in range(1, NX)]
    came, kernels = lax.optimization_barrier((came, kernels))

    give = [jnp.where(first, came[j][:, 1], came[j][:, 0]) for j in range(1, far)]
    give.append(jnp.where(first, came[far][1], came[far][0])[None])
    got = swap(jnp.concatenate(give))

    own, *sends, held, mine = call(
        first_kernel,
        [(plane, F32)] + [(plane, BF16)] * (NX - 1) + [((NX, taps, group), BF16), ((NZ,) + plane, BF16)],
        [((NX * 9 * width, 2 * group), BF16), ((2 * group, PLANE), BF16), ((NX * 9 * width, PLANE), F32)],
        "conv_in", work, at, pair, other, *[came[j] for j in range(1, far)], came[far], got, *kernels,
    )
    sends = [around(sends[k - 1], "x", NX - k) for k in (2, 1, 3)]
    own = own + sum(part.astype(F32) for part in sends)
    held, across = swap(held), swap(mine)

    (send,) = call(act_kernel, [(plane, BF16)], [], "act", 0, at, own, swap(own))
    acts = {k: around(send, "x", k) for k in (1, 3, 2)}
    zero, hold, half, give, grads = call(
        second_kernel,
        [(plane, BF16), ((far - 1,) + plane, BF16), (plane[1:], BF16), ((NZ - 1,) + plane[1:], BF16), ((4 * NX,) + piece, BF16)],
        [((NX * 18 * width, PLANE), BF16), ((NX * 18 * width, group), BF16), ((2 * group, PLANE), BF16), ((NZ,) + plane, BF16)],
        "conv_out", 2 * work, at, send, acts[1], acts[3], acts[2], held, across,
    )
    grads = lax.all_to_all(grads, ("samples", "x"), 0, 0, tiled=True)
    got = swap(give)
    sends = [jnp.stack([hold[j - 1], got[2 * j - 2 : 2 * j]]) for j in range(1, far)] + [jnp.stack([half, got[NZ - 2]])]
    came = {j: apart(sends[j - 1], j) for j in range(far, 0, -1)}
    summed = jnp.sum(grads.reshape((4, NX) + piece).astype(F32), axis=0).astype(BF16)
    summed, came[far] = lax.optimization_barrier((summed, came[far]))
    pieces = {k: around(summed, "samples", k) for k in (1, 3, 2)}
    pieces = [summed] + [pieces[k] for k in (1, 3, 2)]
    pieces, came = lax.optimization_barrier((pieces, came))
    others = swap(jnp.stack(pieces))
    keep, give = call(
        sum_kernel, [(plane, F32), (plane, BF16)], [], "sum", 0, at, *[came[j] for j in range(1, far)], came[far], zero
    )
    got = swap(give)
    scratch = [((28 * width, channels), BF16), ((taps, channels), F32)]
    weights = [((taps, channels), F32)] * 2
    grads = call(
        own_kernel, weights, scratch + [pltpu.SemaphoreType.DMA((3,))], "finish_own", 4 * taps * channels * channels,
        at, *pieces, order, out_space=pl.ANY,
    )
    mixed_out, input_grad, grad_one, grad_two = call(
        finish_kernel, [((width, PLANE), BF16)] * 2 + weights,
        scratch + [(plane, BF16), pltpu.SemaphoreType.DMA((5,))],
        "finish", 0, at, others, keep, got, order, *grads, out_space=pl.ANY, within=2,
    )
    shape = (width, 1, 1, PLANE)
    weights = (27, width, channels)
    return mixed_out.reshape(shape), input_grad.reshape(shape), grad_one.reshape(weights), grad_two.reshape(weights)


def solution(mesh):
    fine = Mesh(
        mesh.devices.reshape(mesh.shape["samples"], NZ, NX, mesh.shape["spatial"]),
        ("samples", "z", "x", "spatial"),
    )
    acts = P(("z", "x"), "samples", "spatial", None)
    kernels = P(None, ("z", "x"), None)
    return jax.shard_map(
        body,
        mesh=fine,
        in_specs=(acts, kernels, kernels, acts),
        out_specs=(acts, acts, kernels, kernels),
        check_vma=False,
    )
```
